32 devices in a mesh: groups: 2 (over x), section: 16 (over z, y, core).
Axes of the slice: x: 2, y: 2, z: 4, core: 2. Of those that a mesh axis runs over, the one named last changes fastest.
Arguments:
- queries: bfloat16 [4096, 4096], P(('groups', 'section')), parts along dimension 0, may hold values from -400 to 400
- keys: bfloat16 [4096, 256], P(('groups', 'section')), parts along dimension 0, may hold values from -4 to 4
- values: bfloat16 [4096, 256], P(('groups', 'section')), parts along dimension 0, may hold values from -6 to 6
- windows: int32 [32], P('groups'), parts along dimension 0, may hold values from 0 to 1024, as said below
Outputs:
- attended: bfloat16 [4096, 4096], P(('groups', 'section')), parts along dimension 0
- log_total: float32 [4096, 32], P(('groups', 'section')), parts along dimension 0
The draws below stay inside these ranges and needn't reach their ends.
There are 2 independent parts, one for each index of `groups`. The reference program is written for one: setup_inputs(seed, part) draws one part's arguments, and reference() takes and returns one part's arrays. A program takes and returns all parts, laid end to end along the dimension named above; each array names one. Nothing has to cross between parts.
Inputs may be any that keep to these rules, and one draw needn't show every extreme that they name: `windows`: the first slice's window is 0 and the last slice's window is 1024.
All inputs are finite; a program needn't handle non-finite values.
Results may differ from the reference program's by a relative error of at most 0.0055.
Values may be sent and summed in bfloat16 or wider, within the bound.
No kernel may reach another device: no remote copies, remote signals or barrier semaphores. Data moves between devices by JAX's collectives and lax.ppermute only.
A program may use at most 64 MiB of HBM per device.

```python
import jax
import jax.numpy as jnp
from jax import lax

QH = 32
KVH = 2
HD = 128
SR = 128
WMAX = 1024
S = 2048
N_SECTION = 16


def make_pair(key):
    token_count = SR * N_SECTION
    key_q = jax.random.fold_in(key, 101)
    key_k = jax.random.fold_in(key, 102)
    base_q = jnp.clip(jax.random.normal(key_q, (token_count, QH, HD), jnp.float32), -4.0, 4.0)
    base_k = jnp.clip(jax.random.normal(key_k, (token_count, KVH, HD), jnp.float32), -4.0, 4.0)
    return (base_q.reshape(token_count, QH * HD), base_k.reshape(token_count, KVH * HD))


def draw_queries(key, part):
    return make_pair(key)[0].astype(jnp.bfloat16)


def draw_keys(key, part):
    return make_pair(key)[1].astype(jnp.bfloat16)


def draw_windows(key, part):
    key_base = jax.random.fold_in(key, 201)
    key_full = jax.random.fold_in(key, 202)
    base = jax.random.randint(key_base, (N_SECTION,), 0, WMAX + 1)
    full = jax.random.randint(key_full, (N_SECTION,), 0, 4) == 0
    position = jnp.arange(N_SECTION)
    full = full | (position == N_SECTION - 1)
    chosen = jnp.where(full, WMAX, base)
    chosen = jnp.where(position == 0, 0, chosen)
    return chosen.astype(jnp.int32)


def level_of(key, extent, split, low, top_value):
    gain = 1.0
    for dim, blocks in split:
        draws = jax.random.uniform(jax.random.fold_in(jax.random.fold_in(key, 6), dim), (blocks,), jnp.float32, low / len(split), top_value / len(split))
        gain = gain * jnp.repeat(jnp.exp(draws), extent[dim] // blocks).reshape((-1,) + (1,) * (len(extent) - 1 - dim))
    return gain


def normal_values(stream_key, dims, width, most, split=(), kind=jnp.bfloat16):
    entries = width * jax.random.normal(stream_key, dims, jnp.float32)
    if split:
        entries = entries * level_of(stream_key, dims, split, -0.22, 0.18)
    return jnp.clip(entries, -most, most).astype(kind)


def setup_inputs(seed: int = 0, part: int = 0) -> dict:
    streams_of = jax.random.split(jax.random.key(seed), 5)
    own_keys = jax.random.split(jax.random.fold_in(streams_of[4], part), 5)
    return {
        "queries": draw_queries(jax.random.fold_in(jax.random.fold_in(streams_of[4], part), 71), part),
        "keys": draw_keys(jax.random.fold_in(jax.random.fold_in(streams_of[4], part), 71), part),
        "values": normal_values(own_keys[2], (S, KVH * HD), 1.0, 6.0, ((0, 16),)),
        "windows": draw_windows(jax.random.fold_in(jax.random.fold_in(streams_of[4], part), 71), part),
    }


def reference(queries, keys, values, windows):
    per_group = QH // KVH
    scale = HD ** -0.5
    span = WMAX + SR
    padded_keys = jnp.concatenate([jnp.zeros((WMAX, KVH * HD), keys.dtype), keys], 0)
    padded_values = jnp.concatenate([jnp.zeros((WMAX, KVH * HD), values.dtype), values], 0)

    def one_slice(index):
        row_start = (index * SR).astype(jnp.int32)
        block_q = lax.dynamic_slice_in_dim(queries, row_start, SR, 0).reshape(SR, KVH, per_group, HD).astype(jnp.float32)
        block_k = lax.dynamic_slice_in_dim(padded_keys, row_start, span, 0).reshape(span, KVH, HD).astype(jnp.float32)
        block_v = lax.dynamic_slice_in_dim(padded_values, row_start, span, 0).reshape(span, KVH, HD).astype(jnp.float32)
        scores = jnp.einsum('rgjd,ngd->gjrn', block_q, block_k) * scale
        key_pos = row_start - WMAX + jnp.arange(span, dtype=jnp.int32)
        row_pos = row_start + jnp.arange(SR, dtype=jnp.int32)
        lowest = row_start - windows[index]
        visible = (key_pos[None, :] >= lowest) & (key_pos[None, :] >= 0) & (key_pos[None, :] <= row_pos[:, None])
        scores = jnp.where(visible, scores, jnp.float32(-1e30))
        row_max = jnp.max(scores, -1)
        expos = jnp.where(visible, jnp.exp(scores - row_max[..., None]), jnp.float32(0.0))
        total = jnp.sum(expos, -1)
        rounded = lax.optimization_barrier(expos.astype(jnp.bfloat16)).astype(jnp.float32)
        summed = jnp.einsum('gjrn,ngd->rgjd', rounded, block_v)
        output = (summed / jnp.transpose(total, (2, 0, 1))[..., None]).reshape(SR, QH * HD).astype(jnp.bfloat16)
        log_sum = jnp.transpose(row_max + jnp.log(total), (2, 0, 1)).reshape(SR, QH)
        return output, log_sum

    outputs, log_sums = lax.map(one_slice, jnp.arange(N_SECTION, dtype=jnp.int32))
    return outputs.reshape(N_SECTION * SR, QH * HD), log_sums.reshape(N_SECTION * SR, QH)
```

```python
import functools
import math

import jax
import jax.numpy as jnp
from jax import lax
from jax.experimental import pallas as pl
from jax.experimental.pallas import tpu as pltpu
from jax.sharding import PartitionSpec as P

HD = 128
SCALE = HD ** (-0.5)
TO_EXP2 = SCALE * math.log2(math.e)
HIDDEN = -1e30


def shifted(block, axis, distance):
    size = lax.axis_size(axis)
    return lax.ppermute(block, axis, [(i, (i + distance) % size) for i in range(size)])


def swapped(block, axis):
    return lax.ppermute(block, axis, [(i ^ 1, i) for i in range(lax.axis_size(axis))])


def head_rows(q_ref):
    heads = q_ref.shape[1] // HD
    return jnp.concatenate([q_ref[:, h * HD : (h + 1) * HD] for h in range(heads)], 0)


def scores_of(key_rows, query_rows):
    return lax.dot_general(
        key_rows, query_rows, (((1,), (1,)), ((), ())), preferred_element_type=jnp.float32
    )


def weighted(value_rows, weights):
    return lax.dot_general(
        value_rows,
        weights.astype(jnp.bfloat16),
        (((0,), (0,)), ((), ())),
        preferred_element_type=jnp.float32,
    )


def finish(summed, top, total, out_ref, log_ref, log_scratch):
    heads = out_ref.shape[1] // HD
    result = summed * (1.0 / total)
    for h in range(heads):
        out_ref[:, h * HD : (h + 1) * HD] = result[:, h * HD : (h + 1) * HD].T.astype(
            out_ref.dtype
        )
    logs = top * SCALE + jnp.log(total)
    group = pl.program_id(0)
    log_scratch[pl.ds(group * heads, heads), :] = jnp.concatenate(
        [logs[:, h * HD : (h + 1) * HD] for h in range(heads)], 0
    )

    @pl.when(group == pl.num_programs(0) - 1)
    def _():
        log_ref[...] = log_scratch[...].T


def near_kernel(axis, win_ref, q_ref, k0, v0, k1, v1, sum_ref, stat_ref):
    me = lax.axis_index(axis)
    rows = k0.shape[0]
    lowest = jnp.maximum(rows - win_ref[me], 0)
    query_rows = head_rows(q_ref)
    count = query_rows.shape[0]
    keys = jnp.concatenate([k1[...], k0[...]], 0)
    values = jnp.concatenate([v1[...], v0[...]], 0)
    scores = scores_of(keys, query_rows)
    key_pos = lax.broadcasted_iota(jnp.int32, (2 * rows, rows), 0)
    row_pos = lax.broadcasted_iota(jnp.int32, (2 * rows, rows), 1) + rows
    odd = (me & 1) == 1
    start = jnp.where(odd, lowest, rows)
    visible = (key_pos >= start) & (key_pos <= row_pos)
    bias = jnp.where(visible, 0.0, HIDDEN)
    scores = scores + jnp.concatenate([bias] * (count // rows), 1)
    top = jnp.max(scores, 0, keepdims=True)
    weights = jnp.exp2((scores - top) * TO_EXP2)
    stat_ref[0:1] = top
    stat_ref[1:2] = jnp.sum(weights, 0, keepdims=True)
    sum_ref[...] = weighted(values, weights)


def far_kernel(axis, distances, last, win_ref, q_ref, *refs):
    me = lax.axis_index(axis)
    sibling = me ^ 1
    pieces = 2 * len(distances)
    key_refs, value_refs = refs[:pieces], refs[pieces : 2 * pieces]
    sum_in, stat_in = refs[2 * pieces : 2 * pieces + 2]
    outs = refs[2 * pieces + 2 :]
    rows = key_refs[0].shape[0]
    lowest = jnp.maximum(me * rows - win_ref[me], 0)
    starts = [(who - d) * rows for d in distances for who in (me, sibling)]
    needed = functools.reduce(jnp.logical_or, [s + rows > lowest for s in starts])

    def emit(summed, top, total):
        if last:
            finish(summed, top, total, *outs)
        else:
            outs[0][...] = summed
            outs[1][0:1] = top
            outs[1][1:2] = total

    @pl.when(needed)
    def _():
        query_rows = head_rows(q_ref)
        keys = jnp.concatenate([r[...] for r in key_refs], 0)
        values = jnp.concatenate([r[...] for r in value_refs], 0)
        scores = scores_of(keys, query_rows)
        local = lax.broadcasted_iota(jnp.int32, (rows, 1), 0)
        key_pos = jnp.concatenate([local + s for s in starts], 0)
        scores = jnp.where(key_pos >= lowest, scores, HIDDEN)
        old_top, old_total = stat_in[0:1], stat_in[1:2]
        top = jnp.maximum(old_top, jnp.max(scores, 0, keepdims=True))
        factor = jnp.exp2((old_top - top) * TO_EXP2)
        weights = jnp.exp2((scores - top) * TO_EXP2)
        total = old_total * factor + jnp.sum(weights, 0, keepdims=True)
        emit(sum_in[...] * factor + weighted(values, weights), top, total)

    @pl.when(jnp.logical_not(needed))
    def _():
        emit(sum_in[...], stat_in[0:1], stat_in[1:2])


def attend(kernel, axis, windows, queries, blocks, state, last):
    rows, width = queries.shape
    groups = blocks[0].shape[1] // (2 * HD)
    wide = width // groups
    whole = lambda g, w: (0, 0)
    mine = lambda g, w: (0, g)
    values = lambda g, w: (0, groups + g)
    state_shapes = [
        jax.ShapeDtypeStruct((HD, width), jnp.float32),
        jax.ShapeDtypeStruct((2, width), jnp.float32),
    ]
    state_specs = [pl.BlockSpec((HD, wide), mine), pl.BlockSpec((2, wide), mine)]
    heads = width // HD
    if last:
        out_shape = [
            jax.ShapeDtypeStruct((rows, width), jnp.bfloat16),
            jax.ShapeDtypeStruct((rows, heads), jnp.float32),
        ]
        out_specs = [pl.BlockSpec((rows, wide), mine), pl.BlockSpec((rows, heads), whole)]
        scratch = [pltpu.VMEM((heads, rows), jnp.float32)]
    else:
        out_shape, out_specs, scratch = state_shapes, state_specs, []
    keys_spec = pl.BlockSpec((rows, HD), mine)
    values_spec = pl.BlockSpec((rows, HD), values)
    count = len(blocks)
    if kernel is near_kernel:
        operands = [x for b in blocks for x in (b, b)]
        specs = [keys_spec, values_spec] * count
    else:
        operands = list(blocks) * 2
        specs = [keys_spec] * count + [values_spec] * count
    aliases = {}
    if state is not None:
        if not last:
            aliases = {2 + len(operands): 0, 3 + len(operands): 1}
        operands += list(state)
        specs += state_specs
    flops = 4 * count * rows * rows * width
    return pl.pallas_call(
        kernel if kernel is not near_kernel else functools.partial(near_kernel, axis),
        grid_spec=pltpu.PrefetchScalarGridSpec(
            num_scalar_prefetch=1,
            grid=(groups,),
            in_specs=[pl.BlockSpec((rows, wide), mine)] + specs,
            out_specs=out_specs,
            scratch_shapes=scratch,
        ),
        out_shape=out_shape,
        input_output_aliases=aliases,
        cost_estimate=pl.CostEstimate(
            flops=flops,
            bytes_accessed=rows * width * 2,
            transcendentals=count * rows * rows * width // HD,
        ),
        compiler_params=pltpu.CompilerParams(vmem_limit_bytes=40 << 20),
    )(windows, queries, *operands)


def on_device(queries, keys, values, windows):
    axis = "section"
    reach = lax.axis_size(axis) // 2
    own = jnp.concatenate([keys, values], 1)
    state = attend(
        near_kernel, axis, windows, queries, [own, swapped(own, axis)], None, False
    )
    held = {4: shifted(own, axis, 4), 2: shifted(own, axis, 2)}
    for first in range(2, reach + 1, 4):
        distances = [d for d in (first, first + 2) if d <= reach]
        last = first + 4 > reach
        blocks = [x for d in distances for x in (held[d], swapped(held[d], axis))]
        if not last:
            for d in (first + 6, first + 4):
                if d <= reach:
                    held[d] = shifted(held[d - 4], axis, 4)
        state = attend(
            functools.partial(far_kernel, axis, distances, last),
            axis,
            windows,
            queries,
            blocks,
            state,
            last,
        )
    return tuple(state)


def solution(mesh):
    placed = (
        P(("groups", "section"), None),
        P(("groups", "section"), None),
        P(("groups", "section"), None),
        P("groups"),
    )
    return jax.shard_map(
        on_device,
        mesh=mesh,
        in_specs=placed,
        out_specs=(P(("groups", "section"), None), P(("groups", "section"), None)),
        check_vma=False,
    )
```

```python
import functools
import math

import jax
import jax.numpy as jnp
from jax import lax
from jax.experimental import pallas as pl
from jax.experimental.pallas import tpu as pltpu
from jax.sharding import PartitionSpec as P

HD = 128
SCALE = HD ** (-0.5)
TO_EXP2 = SCALE * math.log2(math.e)
HIDDEN = -1e30
SUM_ROWS = 8
STATE_ROWS = HD + 2 * SUM_ROWS
TOP_ROW = HD + SUM_ROWS
TILE = 64
VMEM = pl.BlockSpec(memory_space=pltpu.VMEM)
ANY = pl.BlockSpec(memory_space=pl.ANY)
SMEM = pl.BlockSpec(memory_space=pltpu.SMEM)


def shifted(block, axis, distance):
    size = lax.axis_size(axis)
    return lax.ppermute(block, axis, [(i, (i + distance) % size) for i in range(size)])


def swapped(block, axis):
    return lax.ppermute(block, axis, [(i ^ 1, i) for i in range(lax.axis_size(axis))])


def dot(left, right, dims):
    return lax.dot_general(left, right, (dims, ((), ())), preferred_element_type=jnp.float32)


def run_chunks(q_ref, blocks, flags, row_flags, state_in, state_out, s_buf, p_buf, out_ref, log_ref):
    rows, width = q_ref.shape
    groups = blocks[0].shape[1] // (2 * HD)
    slots, keys, wide = s_buf.shape
    heads = wide // HD
    chunks = width // wide
    per_group = chunks // groups
    row_part = jnp.concatenate([row_flags] * heads, 0)
    ones = jnp.ones((2 * SUM_ROWS, keys), jnp.bfloat16)
    key_ext, value_ext = [], []
    for g in range(groups):
        key_rows = jnp.concatenate([b[:, g * HD : (g + 1) * HD] for b in blocks], 0)
        value_rows = jnp.concatenate(
            [b[:, (groups + g) * HD : (groups + g + 1) * HD] for b in blocks], 0
        )
        key_ext.append(jnp.concatenate([key_rows, flags], 1))
        value_ext.append(jnp.concatenate([value_rows.T, ones], 0))

    def score(c):
        parts = [q_ref[:, c * wide + h * HD : c * wide + (h + 1) * HD] for h in range(heads)]
        query_rows = jnp.concatenate([jnp.concatenate(parts, 0), row_part], 1)
        s_buf[c % slots] = dot(key_ext[c // per_group], query_rows, ((1,), (1,)))

    def weigh(c):
        slot, step = c % slots, min(2 * HD, wide)
        tops, factors = [], []
        for j in range(0, wide, step):
            tiles = [
                (k, slice(j, j + step)) for k in range(0, keys, TILE)
            ]
            top = None
            for k, lanes in tiles:
                part = s_buf[slot, k : k + TILE, lanes].reshape(TILE // 8, 8, step)
                part = jnp.max(part, 0)
                top = part if top is None else jnp.maximum(top, part)
            top = jnp.max(top, 0, keepdims=True)
            if state_in is not None:
                old = state_in[TOP_ROW : TOP_ROW + 1, c * wide + j : c * wide + j + step]
                top = jnp.maximum(top, old)
                factors.append(jnp.exp2((old - top) * TO_EXP2))
            for k, lanes in tiles:
                weights = jnp.exp2((s_buf[slot, k : k + TILE, lanes] - top) * TO_EXP2)
                p_buf[slot, k : k + TILE, lanes] = weights.astype(jnp.bfloat16)
            tops.append(top)
        top = jnp.concatenate(tops, 1)
        return top, (jnp.concatenate(factors, 1) if factors else None)

    def sum_up(c, top, factor):
        lanes = slice(c * wide, (c + 1) * wide)
        summed = dot(value_ext[c // per_group], p_buf[c % slots], ((1,), (0,)))[:TOP_ROW]
        if factor is not None:
            summed = summed + state_in[0:TOP_ROW, lanes] * factor
        if out_ref is None:
            state_out[0:TOP_ROW, lanes] = summed
            state_out[TOP_ROW : TOP_ROW + 1, lanes] = top
        else:
            finish(summed, top, c, heads, out_ref, log_ref)

    held = {}
    for t in range(chunks + 2):
        if t < chunks:
            score(t)
        if 0 <= t - 1 < chunks:
            held[t - 1] = weigh(t - 1)
        if 0 <= t - 2 < chunks:
            sum_up(t - 2, *held.pop(t - 2))


def finish(summed, top, c, heads, out_ref, log_ref):
    total = summed[HD : HD + 1]
    result = summed[:HD] * (1.0 / total)
    logs = top * SCALE + jnp.log(total)
    first = c * heads
    for h in range(heads):
        lanes = slice(h * HD, (h + 1) * HD)
        out_ref[:, (first + h) * HD : (first + h + 1) * HD] = result[:, lanes].T.astype(
            out_ref.dtype
        )
    log_ref[first : first + heads, :] = jnp.concatenate(
        [logs[:, h * HD : (h + 1) * HD] for h in range(heads)], 0
    )


def lane_row(rows):
    lane = lax.broadcasted_iota(jnp.int32, (rows, HD), 1)
    row = lax.broadcasted_iota(jnp.int32, (rows, HD), 0)
    return lane, row


def near_kernel(axis, win_ref, q_ref, own, other, state_out, s_buf, p_buf):
    me = lax.axis_index(axis)
    rows = own.shape[0]
    lane, row = lane_row(rows)
    first_seen = jnp.where((me & 1) == 1, jnp.maximum(rows - win_ref[me], 0), rows)
    other_flags = jnp.where((lane == 0) & (row < first_seen), 1.0, 0.0)
    own_flags = jnp.where((lane == row) & (row > 0), 1.0, 0.0)
    flags = jnp.concatenate([other_flags, own_flags], 0).astype(jnp.bfloat16)
    row_flags = jnp.where((lane == 0) | (lane > row), HIDDEN, 0.0).astype(jnp.bfloat16)
    run_chunks(
        q_ref, [other, own], flags, row_flags, None, state_out, s_buf, p_buf, None, None
    )


def far_kernel(axis, distances, last, win_ref, q_ref, *refs):
    me = lax.axis_index(axis)
    count = 2 * len(distances)
    blocks, state_in = refs[:count], refs[count]
    if last:
        state_out, (out_ref, log_ref, s_buf, p_buf) = None, refs[count + 1 :]
    else:
        (state_out, s_buf, p_buf), out_ref, log_ref = refs[count + 1 :], None, None
    rows = blocks[0].shape[0]
    lowest = jnp.maximum(me * rows - win_ref[me], 0)
    starts = [(who - d) * rows for d in distances for who in (me, me ^ 1)]
    needed = functools.reduce(jnp.logical_or, [s + rows > lowest for s in starts])

    @pl.when(needed)
    def _():
        lane, row = lane_row(rows)
        flags = jnp.concatenate(
            [jnp.where((lane == 0) & (row + s < lowest), 1.0, 0.0) for s in starts], 0
        ).astype(jnp.bfloat16)
        row_flags = jnp.where(lane == 0, HIDDEN, 0.0).astype(jnp.bfloat16)
        run_chunks(
            q_ref, blocks, flags, row_flags, state_in, state_out, s_buf, p_buf, out_ref, log_ref
        )

    @pl.when(jnp.logical_not(needed))
    def _():
        if last:
            wide = s_buf.shape[2]
            for c in range(q_ref.shape[1] // wide):
                lanes = slice(c * wide, (c + 1) * wide)
                top = state_in[TOP_ROW : TOP_ROW + 1, lanes]
                finish(state_in[0:TOP_ROW, lanes], top, c, wide // HD, out_ref, log_ref)
        else:
            state_out[...] = state_in[...]


def attend(kernel, windows, queries, blocks, state, last):
    rows, width = queries.shape
    heads = width // HD
    groups = blocks[0].shape[1] // (2 * HD)
    wide = HD * math.gcd(heads // groups, 4)
    keys = len(blocks) * rows
    operands = [windows, queries, *blocks]
    aliases = {}
    if state is not None:
        if not last:
            aliases = {len(operands): 0}
        operands.append(state)
    if last:
        out_shape = [
            jax.ShapeDtypeStruct((rows, width), jnp.bfloat16),
            jax.ShapeDtypeStruct((heads, rows), jnp.float32),
        ]
    else:
        out_shape = [jax.ShapeDtypeStruct((STATE_ROWS, width), jnp.float32)]
    return pl.pallas_call(
        kernel,
        in_specs=[SMEM] + [VMEM] * (len(operands) - 1),
        out_specs=[VMEM] * len(out_shape),
        out_shape=out_shape,
        scratch_shapes=[
            pltpu.VMEM((2, keys, wide), jnp.float32),
            pltpu.VMEM((2, keys, wide), jnp.bfloat16),
        ],
        input_output_aliases=aliases,
        cost_estimate=pl.CostEstimate(
            flops=4 * keys * rows * width,
            bytes_accessed=rows * width * 2,
            transcendentals=keys * rows * heads,
        ),
        compiler_params=pltpu.CompilerParams(vmem_limit_bytes=32 << 20),
    )(*operands)


def pack_kernel(k_ref, v_ref, out_ref):
    width = k_ref.shape[1]
    out_ref[:, :width] = k_ref[...]
    out_ref[:, width:] = v_ref[...]


def packed(keys, values):
    rows, width = keys.shape
    return pl.pallas_call(
        pack_kernel,
        in_specs=[VMEM] * 2,
        out_specs=VMEM,
        out_shape=jax.ShapeDtypeStruct((rows, 2 * width), keys.dtype),
    )(keys, values)


def tied(block, earlier):
    def kernel(block_ref, earlier_ref, out_ref):
        pass

    return pl.pallas_call(
        kernel,
        in_specs=[ANY, ANY],
        out_specs=ANY,
        out_shape=jax.ShapeDtypeStruct(block.shape, block.dtype),
        input_output_aliases={0: 0},
    )(block, earlier)


def on_device(queries, keys, values, windows):
    axis = "section"
    reach = lax.axis_size(axis) // 2
    own = packed(keys, values)
    other = swapped(own, axis)
    held = {4: shifted(own, axis, 4), 2: shifted(own, axis, 2)}
    (state,) = attend(
        functools.partial(near_kernel, axis), windows, queries, [own, other], None, False
    )
    for first in range(2, reach + 1, 4):
        distances = [d for d in (first + 2, first) if d <= reach]
        last = first + 4 > reach
        blocks = []
        for d in distances:
            held[d] = tied(held[d], state)
            if d + 4 <= reach:
                held[d + 4] = shifted(held[d], axis, 4)
            blocks += [held[d], swapped(held[d], axis)]
        result = attend(
            functools.partial(far_kernel, axis, distances, last),
            windows,
            queries,
            blocks,
            state,
            last,
        )
        state = result[0]
    return result[0], result[1].T


def solution(mesh):
    placed = (
        P(("groups", "section"), None),
        P(("groups", "section"), None),
        P(("groups", "section"), None),
        P("groups"),
    )
    return jax.shard_map(
        on_device,
        mesh=mesh,
        in_specs=placed,
        out_specs=(P(("groups", "section"), None), P(("groups", "section"), None)),
        check_vma=False,
    )
```

```python
import functools
import math

import jax
import jax.numpy as jnp
from jax import lax
from jax.experimental import pallas as pl
from jax.experimental.pallas import tpu as pltpu
from jax.sharding import PartitionSpec as P

HD = 128
SCALE = HD ** (-0.5)
TO_EXP2 = SCALE * math.log2(math.e)
HIDDEN = -1e30
SUM_ROWS = 8
STATE_ROWS = HD + 2 * SUM_ROWS
TOP_ROW = HD + SUM_ROWS
TILE = 64
VMEM = pl.BlockSpec(memory_space=pltpu.VMEM)
SMALL = pltpu.CompilerParams(vmem_limit_bytes=1 << 20)
SMEM = pl.BlockSpec(memory_space=pltpu.SMEM)
HBM = pl.BlockSpec(memory_space=pltpu.HBM)
MARK = (8, HD)


def shifted(block, axis, distance):
    size = lax.axis_size(axis)
    return lax.ppermute(block, axis, [(i, (i + distance) % size) for i in range(size)])


def swapped(block, axis):
    return lax.ppermute(block, axis, [(i ^ 1, i) for i in range(lax.axis_size(axis))])


def dot(left, right, dims):
    return lax.dot_general(left, right, (dims, ((), ())), preferred_element_type=jnp.float32)


def run_chunks(q_ref, blocks, flags, row_flags, state_in, state_out, s_buf, p_buf, out_ref, log_ref):
    rows, width = q_ref.shape
    groups = blocks[0].shape[1] // (2 * HD)
    slots, keys, wide = s_buf.shape
    heads = wide // HD
    chunks = width // wide
    per_group = chunks // groups
    row_part = jnp.concatenate([row_flags] * heads, 0)
    ones = jnp.ones((2 * SUM_ROWS, keys), jnp.bfloat16)
    key_ext, value_ext = [], []
    for g in range(groups):
        key_rows = jnp.concatenate([b[:, g * HD : (g + 1) * HD] for b in blocks], 0)
        value_rows = jnp.concatenate(
            [b[:, (groups + g) * HD : (groups + g + 1) * HD] for b in blocks], 0
        )
        key_ext.append(jnp.concatenate([key_rows, flags], 1))
        value_ext.append(jnp.concatenate([value_rows.T, ones], 0))

    def score(c):
        parts = [q_ref[:, c * wide + h * HD : c * wide + (h + 1) * HD] for h in range(heads)]
        query_rows = jnp.concatenate([jnp.concatenate(parts, 0), row_part], 1)
        s_buf[c % slots] = dot(key_ext[c // per_group], query_rows, ((1,), (1,)))

    def weigh(c):
        slot, step = c % slots, min(2 * HD, wide)
        tops, factors = [], []
        for j in range(0, wide, step):
            tiles = [
                (k, slice(j, j + step)) for k in range(0, keys, TILE)
            ]
            top = None
            for k, lanes in tiles:
                part = s_buf[slot, k : k + TILE, lanes].reshape(TILE // 8, 8, step)
                part = jnp.max(part, 0)
                top = part if top is None else jnp.maximum(top, part)
            top = jnp.max(top, 0, keepdims=True)
            if state_in is not None:
                old = state_in[TOP_ROW : TOP_ROW + 1, c * wide + j : c * wide + j + step]
                top = jnp.maximum(top, old)
                factors.append(jnp.exp2((old - top) * TO_EXP2))
            for k, lanes in tiles:
                weights = jnp.exp2((s_buf[slot, k : k + TILE, lanes] - top) * TO_EXP2)
                p_buf[slot, k : k + TILE, lanes] = weights.astype(jnp.bfloat16)
            tops.append(top)
        top = jnp.concatenate(tops, 1)
        return top, (jnp.concatenate(factors, 1) if factors else None)

    def sum_up(c, top, factor):
        lanes = slice(c * wide, (c + 1) * wide)
        summed = dot(value_ext[c // per_group], p_buf[c % slots], ((1,), (0,)))[:TOP_ROW]
        if factor is not None:
            summed = summed + state_in[0:TOP_ROW, lanes] * factor
        if out_ref is None:
            state_out[0:TOP_ROW, lanes] = summed
            state_out[TOP_ROW : TOP_ROW + 1, lanes] = top
        else:
            finish(summed, top, c, heads, out_ref, log_ref)

    held = {}
    for t in range(chunks + 2):
        if t < chunks:
            score(t)
        if 0 <= t - 1 < chunks:
            held[t - 1] = weigh(t - 1)
        if 0 <= t - 2 < chunks:
            sum_up(t - 2, *held.pop(t - 2))


def finish(summed, top, c, heads, out_ref, log_ref):
    total = summed[HD : HD + 1]
    result = summed[:HD] * (1.0 / total)
    logs = top * SCALE + jnp.log(total)
    first = c * heads
    for h in range(heads):
        lanes = slice(h * HD, (h + 1) * HD)
        out_ref[:, (first + h) * HD : (first + h + 1) * HD] = result[:, lanes].T.astype(
            out_ref.dtype
        )
    log_ref[first : first + heads, :] = jnp.concatenate(
        [logs[:, h * HD : (h + 1) * HD] for h in range(heads)], 0
    )


def lane_row(rows):
    lane = lax.broadcasted_iota(jnp.int32, (rows, HD), 1)
    row = lax.broadcasted_iota(jnp.int32, (rows, HD), 0)
    return lane, row


def lowest_of(mark_ref):
    return jnp.max(mark_ref[...]).astype(jnp.int32)


def near_kernel(axis, win_ref, q_ref, own, other, state_out, mark, s_buf, p_buf):
    me = lax.axis_index(axis)
    rows = own.shape[0]
    lowest = jnp.maximum(me * rows - win_ref[me], 0)
    mark[...] = jnp.full(mark.shape, lowest.astype(jnp.float32))
    lane, row = lane_row(rows)
    first_seen = jnp.where((me & 1) == 1, lowest - (me - 1) * rows, rows)
    other_flags = jnp.where((lane == 0) & (row < first_seen), 1.0, 0.0)
    own_flags = jnp.where((lane == row) & (row > 0), 1.0, 0.0)
    flags = jnp.concatenate([other_flags, own_flags], 0).astype(jnp.bfloat16)
    row_flags = jnp.where((lane == 0) | (lane > row), HIDDEN, 0.0).astype(jnp.bfloat16)
    run_chunks(
        q_ref, [other, own], flags, row_flags, None, state_out, s_buf, p_buf, None, None
    )


def far_kernel(axis, distances, last, mark_in, q_ref, *refs):
    me = lax.axis_index(axis)
    count = 2 * len(distances)
    blocks, state_in = refs[:count], refs[count]
    if last:
        state_out, (out_ref, log_ref, s_buf, p_buf) = None, refs[count + 1 :]
    else:
        (state_out, mark, s_buf, p_buf), out_ref, log_ref = refs[count + 1 :], None, None
        mark[...] = mark_in[...]
    rows = blocks[0].shape[0]
    lowest = lowest_of(mark_in)
    starts = [(who - d) * rows for d in distances for who in (me, me ^ 1)]
    needed = functools.reduce(jnp.logical_or, [s + rows > lowest for s in starts])

    @pl.when(needed)
    def _():
        lane, row = lane_row(rows)
        flags = jnp.concatenate(
            [jnp.where((lane == 0) & (row + s < lowest), 1.0, 0.0) for s in starts], 0
        ).astype(jnp.bfloat16)
        row_flags = jnp.where(lane == 0, HIDDEN, 0.0).astype(jnp.bfloat16)
        run_chunks(
            q_ref, blocks, flags, row_flags, state_in, state_out, s_buf, p_buf, out_ref, log_ref
        )

    @pl.when(jnp.logical_not(needed))
    def _():
        if last:
            wide = s_buf.shape[2]
            for c in range(q_ref.shape[1] // wide):
                lanes = slice(c * wide, (c + 1) * wide)
                top = state_in[TOP_ROW : TOP_ROW + 1, lanes]
                finish(state_in[0:TOP_ROW, lanes], top, c, wide // HD, out_ref, log_ref)
        else:
            state_out[...] = state_in[...]


def attend(kernel, mark, queries, blocks, state, last):
    rows, width = queries.shape
    heads = width // HD
    groups = blocks[0].shape[1] // (2 * HD)
    wide = HD * math.gcd(heads // groups, 4)
    keys = len(blocks) * rows
    operands = [mark, queries, *blocks]
    aliases = {}
    if state is not None:
        if not last:
            aliases = {len(operands): 0}
        operands.append(state)
    if last:
        out_shape = [
            jax.ShapeDtypeStruct((rows, width), jnp.bfloat16),
            jax.ShapeDtypeStruct((heads, rows), jnp.float32),
        ]
    else:
        out_shape = [
            jax.ShapeDtypeStruct((STATE_ROWS, width), jnp.float32),
            jax.ShapeDtypeStruct(MARK, jnp.float32),
        ]
    return pl.pallas_call(
        kernel,
        in_specs=[VMEM if state is not None else SMEM] + [VMEM] * (len(operands) - 1),
        out_specs=[VMEM] * len(out_shape),
        out_shape=out_shape,
        scratch_shapes=[
            pltpu.VMEM((2, keys, wide), jnp.float32),
            pltpu.VMEM((2, keys, wide), jnp.bfloat16),
        ],
        input_output_aliases=aliases,
        cost_estimate=pl.CostEstimate(
            flops=4 * keys * rows * width,
            bytes_accessed=rows * width * 2,
            transcendentals=keys * rows * heads,
        ),
        compiler_params=pltpu.CompilerParams(vmem_limit_bytes=12 << 20),
    )(*operands)


def pack_kernel(k_hbm, v_hbm, own_hbm, sems):
    width = k_hbm.shape[1]
    copies = [
        pltpu.make_async_copy(k_hbm, own_hbm.at[:, pl.ds(0, width)], sems.at[0]),
        pltpu.make_async_copy(v_hbm, own_hbm.at[:, pl.ds(width, width)], sems.at[1]),
    ]
    for copy in copies:
        copy.start()
    for copy in copies:
        copy.wait()


def packed(keys, values):
    rows, width = keys.shape
    return pl.pallas_call(
        pack_kernel,
        in_specs=[HBM] * 2,
        out_specs=HBM,
        out_shape=jax.ShapeDtypeStruct((rows, 2 * width), keys.dtype),
        scratch_shapes=[pltpu.SemaphoreType.DMA((2,))],
        compiler_params=pltpu.CompilerParams(vmem_limit_bytes=60 << 20),
    )(keys, values)


def tied(block, earlier):
    def kernel(block_ref, earlier_ref, out_ref):
        pass

    return pl.pallas_call(
        kernel,
        in_specs=[VMEM, VMEM],
        out_specs=VMEM,
        out_shape=jax.ShapeDtypeStruct(block.shape, block.dtype),
        input_output_aliases={0: 0},
        compiler_params=SMALL,
    )(block, earlier)


def on_device(queries, keys, values, windows):
    axis = "section"
    reach = lax.axis_size(axis) // 2
    own = packed(keys, values)
    other = swapped(own, axis)
    held = {4: shifted(own, axis, 4), 2: shifted(own, axis, 2)}
    state, mark = attend(
        functools.partial(near_kernel, axis), windows, queries, [own, other], None, False
    )
    for first in range(2, reach + 1, 4):
        distances = [d for d in (first + 2, first) if d <= reach]
        last = first + 4 > reach
        blocks = []
        for d in distances:
            held[d] = tied(held[d], mark)
            if d + 4 <= reach:
                held[d + 4] = shifted(held[d], axis, 4)
            blocks += [held[d], swapped(held[d], axis)]
        result = attend(
            functools.partial(far_kernel, axis, distances, last),
            mark,
            queries,
            blocks,
            state,
            last,
        )
        state, mark = result
    return result[0], result[1].T


def solution(mesh):
    placed = (
        P(("groups", "section"), None),
        P(("groups", "section"), None),
        P(("groups", "section"), None),
        P("groups"),
    )
    return jax.shard_map(
        on_device,
        mesh=mesh,
        in_specs=placed,
        out_specs=(P(("groups", "section"), None), P(("groups", "section"), None)),
        check_vma=False,
    )
```

```python
import functools
import math

import jax
import jax.numpy as jnp
from jax import lax
from jax.experimental import pallas as pl
from jax.experimental.pallas import tpu as pltpu
from jax.sharding import PartitionSpec as P

HD = 128
SCALE = HD ** (-0.5)
TO_EXP2 = SCALE * math.log2(math.e)
HIDDEN = -1e30
SUM_ROWS = 8
STATE_ROWS = HD + 2 * SUM_ROWS
TOP_ROW = HD + SUM_ROWS
TILE = 64
VMEM = pl.BlockSpec(memory_space=pltpu.VMEM)
SMALL = pltpu.CompilerParams(vmem_limit_bytes=1 << 20)
HBM = pl.BlockSpec(memory_space=pltpu.HBM)
MARK = (8, HD)


def shifted(block, axis, distance):
    size = lax.axis_size(axis)
    return lax.ppermute(block, axis, [(i, (i + distance) % size) for i in range(size)])


def swapped(block, axis):
    return lax.ppermute(block, axis, [(i ^ 1, i) for i in range(lax.axis_size(axis))])


def dot(left, right, dims):
    return lax.dot_general(left, right, (dims, ((), ())), preferred_element_type=jnp.float32)


def run_chunks(q_ref, blocks, flags, row_flags, state_in, state_out, s_buf, p_buf, out_ref, log_ref):
    rows, width = q_ref.shape
    groups = blocks[0].shape[1] // (2 * HD)
    slots, keys, wide = s_buf.shape
    heads = wide // HD
    chunks = width // wide
    per_group = chunks // groups
    row_part = jnp.concatenate([row_flags] * heads, 0)
    ones = jnp.ones((2 * SUM_ROWS, keys), jnp.bfloat16)
    key_ext, value_ext = [], []
    for g in range(groups):
        key_rows = jnp.concatenate([b[:, g * HD : (g + 1) * HD] for b in blocks], 0)
        value_rows = jnp.concatenate(
            [b[:, (groups + g) * HD : (groups + g + 1) * HD] for b in blocks], 0
        )
        key_ext.append(jnp.concatenate([key_rows, flags], 1))
        value_ext.append(jnp.concatenate([value_rows.T, ones], 0))

    def score(c):
        parts = [q_ref[:, c * wide + h * HD : c * wide + (h + 1) * HD] for h in range(heads)]
        query_rows = jnp.concatenate([jnp.concatenate(parts, 0), row_part], 1)
        s_buf[c % slots] = dot(key_ext[c // per_group], query_rows, ((1,), (1,)))

    def weigh(c):
        slot, step = c % slots, min(2 * HD, wide)
        tops, factors = [], []
        for j in range(0, wide, step):
            tiles = [
                (k, slice(j, j + step)) for k in range(0, keys, TILE)
            ]
            top = None
            for k, lanes in tiles:
                part = s_buf[slot, k : k + TILE, lanes].reshape(TILE // 8, 8, step)
                part = jnp.max(part, 0)
                top = part if top is None else jnp.maximum(top, part)
            top = jnp.max(top, 0, keepdims=True)
            if state_in is not None:
                old = state_in[TOP_ROW : TOP_ROW + 1, c * wide + j : c * wide + j + step]
                top = jnp.maximum(top, old)
                factors.append(jnp.exp2((old - top) * TO_EXP2))
            for k, lanes in tiles:
                weights = jnp.exp2((s_buf[slot, k : k + TILE, lanes] - top) * TO_EXP2)
                p_buf[slot, k : k + TILE, lanes] = weights.astype(jnp.bfloat16)
            tops.append(top)
        top = jnp.concatenate(tops, 1)
        return top, (jnp.concatenate(factors, 1) if factors else None)

    def sum_up(c, top, factor):
        lanes = slice(c * wide, (c + 1) * wide)
        summed = dot(value_ext[c // per_group], p_buf[c % slots], ((1,), (0,)))[:TOP_ROW]
        if factor is not None:
            summed = summed + state_in[0:TOP_ROW, lanes] * factor
        if out_ref is None:
            state_out[0:TOP_ROW, lanes] = summed
            state_out[TOP_ROW : TOP_ROW + 1, lanes] = top
        else:
            finish(summed, top, c, heads, out_ref, log_ref)

    held = {}
    for t in range(chunks + 2):
        if t < chunks:
            score(t)
        if 0 <= t - 1 < chunks:
            held[t - 1] = weigh(t - 1)
        if 0 <= t - 2 < chunks:
            sum_up(t - 2, *held.pop(t - 2))


def finish(summed, top, c, heads, out_ref, log_ref):
    total = summed[HD : HD + 1]
    result = summed[:HD] * (1.0 / total)
    logs = top * SCALE + jnp.log(total)
    first = c * heads
    for h in range(heads):
        lanes = slice(h * HD, (h + 1) * HD)
        out_ref[:, (first + h) * HD : (first + h + 1) * HD] = result[:, lanes].T.astype(
            out_ref.dtype
        )
    log_ref[first : first + heads, :] = jnp.concatenate(
        [logs[:, h * HD : (h + 1) * HD] for h in range(heads)], 0
    )


def lane_row(rows):
    lane = lax.broadcasted_iota(jnp.int32, (rows, HD), 1)
    row = lax.broadcasted_iota(jnp.int32, (rows, HD), 0)
    return lane, row


def lowest_of(mark_ref):
    return jnp.max(mark_ref[...]).astype(jnp.int32)


def near_kernel(axis, mark_in, q_ref, own, other, state_out, mark, s_buf, p_buf):
    me = lax.axis_index(axis)
    rows = own.shape[0]
    lowest = lowest_of(mark_in)
    mark[...] = mark_in[...]
    lane, row = lane_row(rows)
    first_seen = jnp.where((me & 1) == 1, lowest - (me - 1) * rows, rows)
    other_flags = jnp.where((lane == 0) & (row < first_seen), 1.0, 0.0)
    own_flags = jnp.where((lane == row) & (row > 0), 1.0, 0.0)
    flags = jnp.concatenate([other_flags, own_flags], 0).astype(jnp.bfloat16)
    row_flags = jnp.where((lane == 0) | (lane > row), HIDDEN, 0.0).astype(jnp.bfloat16)
    run_chunks(
        q_ref, [other, own], flags, row_flags, None, state_out, s_buf, p_buf, None, None
    )


def far_kernel(axis, distances, last, mark_in, q_ref, *refs):
    me = lax.axis_index(axis)
    count = 2 * len(distances)
    blocks, state_in = refs[:count], refs[count]
    if last:
        state_out, (out_ref, log_ref, s_buf, p_buf) = None, refs[count + 1 :]
    else:
        (state_out, mark, s_buf, p_buf), out_ref, log_ref = refs[count + 1 :], None, None
        mark[...] = mark_in[...]
    rows = blocks[0].shape[0]
    lowest = lowest_of(mark_in)
    starts = [(who - d) * rows for d in distances for who in (me, me ^ 1)]
    needed = functools.reduce(jnp.logical_or, [s + rows > lowest for s in starts])

    @pl.when(needed)
    def _():
        lane, row = lane_row(rows)
        flags = jnp.concatenate(
            [jnp.where((lane == 0) & (row + s < lowest), 1.0, 0.0) for s in starts], 0
        ).astype(jnp.bfloat16)
        row_flags = jnp.where(lane == 0, HIDDEN, 0.0).astype(jnp.bfloat16)
        run_chunks(
            q_ref, blocks, flags, row_flags, state_in, state_out, s_buf, p_buf, out_ref, log_ref
        )

    @pl.when(jnp.logical_not(needed))
    def _():
        if last:
            wide = s_buf.shape[2]
            for c in range(q_ref.shape[1] // wide):
                lanes = slice(c * wide, (c + 1) * wide)
                top = state_in[TOP_ROW : TOP_ROW + 1, lanes]
                finish(state_in[0:TOP_ROW, lanes], top, c, wide // HD, out_ref, log_ref)
        else:
            state_out[...] = state_in[...]


def attend(kernel, mark, queries, blocks, state, last):
    rows, width = queries.shape
    heads = width // HD
    groups = blocks[0].shape[1] // (2 * HD)
    wide = HD * math.gcd(heads // groups, 4)
    keys = len(blocks) * rows
    operands = [mark, queries, *blocks]
    aliases = {}
    if state is not None:
        if not last:
            aliases = {len(operands): 0}
        operands.append(state)
    if last:
        out_shape = [
            jax.ShapeDtypeStruct((rows, width), jnp.bfloat16),
            jax.ShapeDtypeStruct((heads, rows), jnp.float32),
        ]
    else:
        out_shape = [
            jax.ShapeDtypeStruct((STATE_ROWS, width), jnp.float32),
            jax.ShapeDtypeStruct(MARK, jnp.float32),
        ]
    return pl.pallas_call(
        kernel,
        in_specs=[VMEM] * len(operands),
        out_specs=[VMEM] * len(out_shape),
        out_shape=out_shape,
        scratch_shapes=[
            pltpu.VMEM((2, keys, wide), jnp.float32),
            pltpu.VMEM((2, keys, wide), jnp.bfloat16),
        ],
        input_output_aliases=aliases,
        cost_estimate=pl.CostEstimate(
            flops=4 * keys * rows * width,
            bytes_accessed=rows * width * 2,
            transcendentals=keys * rows * heads,
        ),
        compiler_params=pltpu.CompilerParams(vmem_limit_bytes=12 << 20),
    )(*operands)


def fetch_kernel(axis, k_hbm, v_hbm, win_hbm, q_hbm, own_ref, mark_ref, q_ref, win_ref, sems):
    rows, width = k_hbm.shape
    copies = [
        pltpu.make_async_copy(k_hbm, own_ref.at[:, pl.ds(0, width)], sems.at[0]),
        pltpu.make_async_copy(v_hbm, own_ref.at[:, pl.ds(width, width)], sems.at[1]),
        pltpu.make_async_copy(win_hbm, win_ref, sems.at[2]),
        pltpu.make_async_copy(q_hbm, q_ref, sems.at[3]),
    ]
    for copy in copies:
        copy.start()
    for copy in copies:
        copy.wait()
    me = lax.axis_index(axis)
    lowest = jnp.maximum(me * rows - win_ref[me], 0)
    mark_ref[...] = jnp.full(mark_ref.shape, lowest.astype(jnp.float32))


def fetched(axis, queries, keys, values, windows):
    rows, width = keys.shape
    sources = [
        pltpu.with_memory_space_constraint(x, pltpu.HBM) for x in (keys, values, windows, queries)
    ]
    return pl.pallas_call(
        functools.partial(fetch_kernel, axis),
        in_specs=[HBM] * 4,
        out_specs=[VMEM] * 3,
        out_shape=[
            jax.ShapeDtypeStruct((rows, 2 * width), keys.dtype),
            jax.ShapeDtypeStruct(MARK, jnp.float32),
            jax.ShapeDtypeStruct(queries.shape, queries.dtype),
        ],
        scratch_shapes=[
            pltpu.SMEM(windows.shape, windows.dtype),
            pltpu.SemaphoreType.DMA((4,)),
        ],
        compiler_params=SMALL,
    )(*sources)


def tied(block, earlier):
    def kernel(block_ref, earlier_ref, out_ref):
        pass

    return pl.pallas_call(
        kernel,
        in_specs=[VMEM, VMEM],
        out_specs=VMEM,
        out_shape=jax.ShapeDtypeStruct(block.shape, block.dtype),
        input_output_aliases={0: 0},
        compiler_params=SMALL,
    )(block, earlier)


def on_device(queries, keys, values, windows):
    axis = "section"
    reach = lax.axis_size(axis) // 2
    own, mark, queries = fetched(axis, queries, keys, values, windows)
    other = swapped(own, axis)
    held = {4: shifted(own, axis, 4), 2: shifted(own, axis, 2)}
    state, mark = attend(
        functools.partial(near_kernel, axis), mark, queries, [own, other], None, False
    )
    for first in range(2, reach + 1, 4):
        distances = [d for d in (first + 2, first) if d <= reach]
        last = first + 4 > reach
        blocks = []
        for d in distances:
            held[d] = tied(held[d], mark)
            if d + 4 <= reach:
                held[d + 4] = shifted(held[d], axis, 4)
            blocks += [held[d], swapped(held[d], axis)]
        result = attend(
            functools.partial(far_kernel, axis, distances, last),
            mark,
            queries,
            blocks,
            state,
            last,
        )
        state, mark = result
    return result[0], result[1].T


def solution(mesh):
    placed = (
        P(("groups", "section"), None),
        P(("groups", "section"), None),
        P(("groups", "section"), None),
        P("groups"),
    )
    return jax.shard_map(
        on_device,
        mesh=mesh,
        in_specs=placed,
        out_specs=(P(("groups", "section"), None), P(("groups", "section"), None)),
        check_vma=False,
    )
```

```python
import functools
import math

import jax
import jax.numpy as jnp
from jax import lax
from jax.experimental import pallas as pl
from jax.experimental.pallas import tpu as pltpu
from jax.sharding import PartitionSpec as P

HD = 128
SCALE = HD ** (-0.5)
TO_EXP2 = SCALE * math.log2(math.e)
HIDDEN = -1e30
SUM_ROWS = 8
STATE_ROWS = HD + 2 * SUM_ROWS
TOP_ROW = HD + SUM_ROWS
TILE = 64
VMEM = pl.BlockSpec(memory_space=pltpu.VMEM)
SMALL = pltpu.CompilerParams(vmem_limit_bytes=1 << 20)
HBM = pl.BlockSpec(memory_space=pltpu.HBM)
MARK = (8, HD)


def reach_of(core, turn):
    return 4 - 2 * (core ^ turn)


def shifted(block, axis, turn):
    size = lax.axis_size(axis)
    return lax.ppermute(
        block, axis, [(i, (i + reach_of(i % 2, turn)) % size) for i in range(size)]
    )


def swapped(block, axis):
    return lax.ppermute(block, axis, [(i ^ 1, i) for i in range(lax.axis_size(axis))])


def dot(left, right, dims):
    return lax.dot_general(left, right, (dims, ((), ())), preferred_element_type=jnp.float32)


def run_chunks(q_ref, blocks, flags, row_flags, state_in, state_out, s_buf, p_buf, out_ref, log_ref):
    rows, width = q_ref.shape
    groups = blocks[0].shape[1] // (2 * HD)
    slots, keys, wide = s_buf.shape
    heads = wide // HD
    chunks = width // wide
    per_group = chunks // groups
    row_part = jnp.concatenate([row_flags] * heads, 0)
    ones = jnp.ones((2 * SUM_ROWS, keys), jnp.bfloat16)
    key_ext, value_ext = [], []
    for g in range(groups):
        key_rows = jnp.concatenate([b[:, g * HD : (g + 1) * HD] for b in blocks], 0)
        value_rows = jnp.concatenate(
            [b[:, (groups + g) * HD : (groups + g + 1) * HD] for b in blocks], 0
        )
        key_ext.append(jnp.concatenate([key_rows, flags], 1))
        value_ext.append(jnp.concatenate([value_rows.T, ones], 0))

    def score(c):
        parts = [q_ref[:, c * wide + h * HD : c * wide + (h + 1) * HD] for h in range(heads)]
        query_rows = jnp.concatenate([jnp.concatenate(parts, 0), row_part], 1)
        s_buf[c % slots] = dot(key_ext[c // per_group], query_rows, ((1,), (1,)))

    def weigh(c):
        slot, step = c % slots, min(2 * HD, wide)
        tops, factors = [], []
        for j in range(0, wide, step):
            tiles = [
                (k, slice(j, j + step)) for k in range(0, keys, TILE)
            ]
            top = None
            for k, lanes in tiles:
                part = s_buf[slot, k : k + TILE, lanes].reshape(TILE // 8, 8, step)
                part = jnp.max(part, 0)
                top = part if top is None else jnp.maximum(top, part)
            top = jnp.max(top, 0, keepdims=True)
            if state_in is not None:
                old = state_in[TOP_ROW : TOP_ROW + 1, c * wide + j : c * wide + j + step]
                top = jnp.maximum(top, old)
                factors.append(jnp.exp2((old - top) * TO_EXP2))
            for k, lanes in tiles:
                weights = jnp.exp2((s_buf[slot, k : k + TILE, lanes] - top) * TO_EXP2)
                p_buf[slot, k : k + TILE, lanes] = weights.astype(jnp.bfloat16)
            tops.append(top)
        top = jnp.concatenate(tops, 1)
        return top, (jnp.concatenate(factors, 1) if factors else None)

    def sum_up(c, top, factor):
        lanes = slice(c * wide, (c + 1) * wide)
        summed = dot(value_ext[c // per_group], p_buf[c % slots], ((1,), (0,)))[:TOP_ROW]
        if factor is not None:
            summed = summed + state_in[0:TOP_ROW, lanes] * factor
        if out_ref is None:
            state_out[0:TOP_ROW, lanes] = summed
            state_out[TOP_ROW : TOP_ROW + 1, lanes] = top
        else:
            finish(summed, top, c, heads, out_ref, log_ref)

    held = {}
    for t in range(chunks + 2):
        if t < chunks:
            score(t)
        if 0 <= t - 1 < chunks:
            held[t - 1] = weigh(t - 1)
        if 0 <= t - 2 < chunks:
            sum_up(t - 2, *held.pop(t - 2))


def finish(summed, top, c, heads, out_ref, log_ref):
    total = summed[HD : HD + 1]
    result = summed[:HD] * (1.0 / total)
    logs = top * SCALE + jnp.log(total)
    first = c * heads
    for h in range(heads):
        lanes = slice(h * HD, (h + 1) * HD)
        out_ref[:, (first + h) * HD : (first + h + 1) * HD] = result[:, lanes].T.astype(
            out_ref.dtype
        )
    log_ref[first : first + heads, :] = jnp.concatenate(
        [logs[:, h * HD : (h + 1) * HD] for h in range(heads)], 0
    )


def lane_row(rows):
    lane = lax.broadcasted_iota(jnp.int32, (rows, HD), 1)
    row = lax.broadcasted_iota(jnp.int32, (rows, HD), 0)
    return lane, row


def lowest_of(mark_ref):
    return jnp.max(mark_ref[...]).astype(jnp.int32)


def near_kernel(axis, mark_in, q_ref, own, other, state_out, mark, s_buf, p_buf):
    me = lax.axis_index(axis)
    rows = own.shape[0]
    lowest = lowest_of(mark_in)
    mark[...] = mark_in[...]
    lane, row = lane_row(rows)
    first_seen = jnp.where((me & 1) == 1, lowest - (me - 1) * rows, rows)
    other_flags = jnp.where((lane == 0) & (row < first_seen), 1.0, 0.0)
    own_flags = jnp.where((lane == row) & (row > 0), 1.0, 0.0)
    flags = jnp.concatenate([other_flags, own_flags], 0).astype(jnp.bfloat16)
    row_flags = jnp.where((lane == 0) | (lane > row), HIDDEN, 0.0).astype(jnp.bfloat16)
    run_chunks(
        q_ref, [other, own], flags, row_flags, None, state_out, s_buf, p_buf, None, None
    )


def far_kernel(axis, level, last, mark_in, q_ref, *refs):
    me = lax.axis_index(axis)
    count = 4
    blocks, state_in = refs[:count], refs[count]
    if last:
        state_out, (out_ref, log_ref, s_buf, p_buf) = None, refs[count + 1 :]
    else:
        (state_out, mark, s_buf, p_buf), out_ref, log_ref = refs[count + 1 :], None, None
        mark[...] = mark_in[...]
    rows = blocks[0].shape[0]
    lowest = lowest_of(mark_in)
    starts = [
        (who - level - reach_of(who & 1, turn)) * rows for turn in (0, 1) for who in (me, me ^ 1)
    ]
    needed = functools.reduce(jnp.logical_or, [s + rows > lowest for s in starts])

    @pl.when(needed)
    def _():
        lane, row = lane_row(rows)
        flags = jnp.concatenate(
            [jnp.where((lane == 0) & (row + s < lowest), 1.0, 0.0) for s in starts], 0
        ).astype(jnp.bfloat16)
        row_flags = jnp.where(lane == 0, HIDDEN, 0.0).astype(jnp.bfloat16)
        run_chunks(
            q_ref, blocks, flags, row_flags, state_in, state_out, s_buf, p_buf, out_ref, log_ref
        )

    @pl.when(jnp.logical_not(needed))
    def _():
        if last:
            wide = s_buf.shape[2]
            for c in range(q_ref.shape[1] // wide):
                lanes = slice(c * wide, (c + 1) * wide)
                top = state_in[TOP_ROW : TOP_ROW + 1, lanes]
                finish(state_in[0:TOP_ROW, lanes], top, c, wide // HD, out_ref, log_ref)
        else:
            state_out[...] = state_in[...]


def attend(kernel, mark, queries, blocks, state, last):
    rows, width = queries.shape
    heads = width // HD
    groups = blocks[0].shape[1] // (2 * HD)
    wide = HD * math.gcd(heads // groups, 4)
    keys = len(blocks) * rows
    operands = [mark, queries, *blocks]
    aliases = {}
    if state is not None:
        if not last:
            aliases = {len(operands): 0}
        operands.append(state)
    if last:
        out_shape = [
            jax.ShapeDtypeStruct((rows, width), jnp.bfloat16),
            jax.ShapeDtypeStruct((heads, rows), jnp.float32),
        ]
    else:
        out_shape = [
            jax.ShapeDtypeStruct((STATE_ROWS, width), jnp.float32),
            jax.ShapeDtypeStruct(MARK, jnp.float32),
        ]
    return pl.pallas_call(
        kernel,
        in_specs=[VMEM] * len(operands),
        out_specs=[VMEM] * len(out_shape),
        out_shape=out_shape,
        scratch_shapes=[
            pltpu.VMEM((2, keys, wide), jnp.float32),
            pltpu.VMEM((2, keys, wide), jnp.bfloat16),
        ],
        input_output_aliases=aliases,
        cost_estimate=pl.CostEstimate(
            flops=4 * keys * rows * width,
            bytes_accessed=rows * width * 2,
            transcendentals=keys * rows * heads,
        ),
        compiler_params=pltpu.CompilerParams(vmem_limit_bytes=12 << 20),
    )(*operands)


def fetch_kernel(axis, k_hbm, v_hbm, win_hbm, q_hbm, own_ref, mark_ref, q_ref, win_ref, sems):
    rows, width = k_hbm.shape
    copies = [
        pltpu.make_async_copy(k_hbm, own_ref.at[:, pl.ds(0, width)], sems.at[0]),
        pltpu.make_async_copy(v_hbm, own_ref.at[:, pl.ds(width, width)], sems.at[1]),
        pltpu.make_async_copy(win_hbm, win_ref, sems.at[2]),
        pltpu.make_async_copy(q_hbm, q_ref, sems.at[3]),
    ]
    for copy in copies:
        copy.start()
    for copy in copies:
        copy.wait()
    me = lax.axis_index(axis)
    lowest = jnp.maximum(me * rows - win_ref[me], 0)
    mark_ref[...] = jnp.full(mark_ref.shape, lowest.astype(jnp.float32))


def fetched(axis, queries, keys, values, windows):
    rows, width = keys.shape
    sources = [
        pltpu.with_memory_space_constraint(x, pltpu.HBM) for x in (keys, values, windows, queries)
    ]
    return pl.pallas_call(
        functools.partial(fetch_kernel, axis),
        in_specs=[HBM] * 4,
        out_specs=[VMEM] * 3,
        out_shape=[
            jax.ShapeDtypeStruct((rows, 2 * width), keys.dtype),
            jax.ShapeDtypeStruct(MARK, jnp.float32),
            jax.ShapeDtypeStruct(queries.shape, queries.dtype),
        ],
        scratch_shapes=[
            pltpu.SMEM(windows.shape, windows.dtype),
            pltpu.SemaphoreType.DMA((4,)),
        ],
        compiler_params=SMALL,
    )(*sources)


def tied(block, mark):
    def kernel(block_ref, mark_ref, out_ref):
        pass

    return pl.pallas_call(
        kernel,
        in_specs=[VMEM, VMEM],
        out_specs=VMEM,
        out_shape=jax.ShapeDtypeStruct(block.shape, block.dtype),
        input_output_aliases={0: 0},
        compiler_params=SMALL,
    )(block, mark)


def choose_kernel(axis, first_ref, second_ref, mark_ref, out_ref):
    odd = (lax.axis_index(axis) & 1) == 1

    @pl.when(odd)
    def _():
        out_ref[...] = second_ref[...]

    @pl.when(jnp.logical_not(odd))
    def _():
        out_ref[...] = first_ref[...]


def chosen(axis, first, second, mark):
    return pl.pallas_call(
        functools.partial(choose_kernel, axis),
        in_specs=[VMEM] * 3,
        out_specs=VMEM,
        out_shape=jax.ShapeDtypeStruct(first.shape, first.dtype),
        compiler_params=SMALL,
    )(first, second, mark)


def on_device(queries, keys, values, windows):
    axis = "section"
    reach = lax.axis_size(axis) // 2
    own, mark, queries = fetched(axis, queries, keys, values, windows)
    other = swapped(own, axis)
    arrived = [shifted(own, axis, turn) for turn in (0, 1)]
    state, mark = attend(
        functools.partial(near_kernel, axis), mark, queries, [own, other], None, False
    )
    for level in range(0, reach, 4):
        last = level + 4 >= reach
        if level:
            arrived = [tied(block, mark) for block in arrived]
        blocks = [x for block in arrived for x in (block, swapped(block, axis))]
        if not last:
            farthest = chosen(axis, *arrived, mark)
            arrived = [shifted(farthest, axis, turn) for turn in (0, 1)]
        result = attend(
            functools.partial(far_kernel, axis, level, last),
            mark,
            queries,
            blocks,
            state,
            last,
        )
        state, mark = result
    return result[0], result[1].T


def solution(mesh):
    placed = (
        P(("groups", "section"), None),
        P(("groups", "section"), None),
        P(("groups", "section"), None),
        P("groups"),
    )
    return jax.shard_map(
        on_device,
        mesh=mesh,
        in_specs=placed,
        out_specs=(P(("groups", "section"), None), P(("groups", "section"), None)),
        check_vma=False,
    )
```

```python
import functools
import math

import jax
import jax.numpy as jnp
from jax import lax
from jax.experimental import pallas as pl
from jax.experimental.pallas import tpu as pltpu
from jax.sharding import PartitionSpec as P

HD = 128
SCALE = HD ** (-0.5)
TO_EXP2 = SCALE * math.log2(math.e)
HIDDEN = -1e30
SUM_ROWS = 8
STATE_ROWS = HD + 2 * SUM_ROWS
TOP_ROW = HD + SUM_ROWS
TILE = 64
VMEM = pl.BlockSpec(memory_space=pltpu.VMEM)
SMALL = pltpu.CompilerParams(vmem_limit_bytes=1 << 20)
HBM = pl.BlockSpec(memory_space=pltpu.HBM)
MARK = (8, HD)


def shifted(block, axis, distance, offset=0):
    size = lax.axis_size(axis)
    route = [(i, i + distance) for i in range(offset, size - distance)]
    route += [(i, i) for i in range(offset)]
    route += [(size - distance + i, offset + i) for i in range(distance)]
    return lax.ppermute(block, axis, sorted(route))


def swapped(block, axis):
    return lax.ppermute(block, axis, [(i ^ 1, i) for i in range(lax.axis_size(axis))])


def dot(left, right, dims):
    return lax.dot_general(left, right, (dims, ((), ())), preferred_element_type=jnp.float32)


def run_chunks(q_ref, blocks, flags, row_flags, state_in, state_out, s_buf, p_buf, out_ref, log_ref):
    rows, width = q_ref.shape
    groups = blocks[0].shape[1] // (2 * HD)
    slots, keys, wide = s_buf.shape
    heads = wide // HD
    chunks = width // wide
    per_group = chunks // groups
    row_part = jnp.concatenate([row_flags] * heads, 0)
    ones = jnp.ones((2 * SUM_ROWS, keys), jnp.bfloat16)
    key_ext, value_ext = [], []
    for g in range(groups):
        key_rows = jnp.concatenate([b[:, g * HD : (g + 1) * HD] for b in blocks], 0)
        value_rows = jnp.concatenate(
            [b[:, (groups + g) * HD : (groups + g + 1) * HD] for b in blocks], 0
        )
        key_ext.append(jnp.concatenate([key_rows, flags], 1))
        value_ext.append(jnp.concatenate([value_rows.T, ones], 0))

    def score(c):
        parts = [q_ref[:, c * wide + h * HD : c * wide + (h + 1) * HD] for h in range(heads)]
        query_rows = jnp.concatenate([jnp.concatenate(parts, 0), row_part], 1)
        s_buf[c % slots] = dot(key_ext[c // per_group], query_rows, ((1,), (1,)))

    def weigh(c):
        slot, step = c % slots, min(2 * HD, wide)
        tops, factors = [], []
        for j in range(0, wide, step):
            tiles = [
                (k, slice(j, j + step)) for k in range(0, keys, TILE)
            ]
            top = None
            for k, lanes in tiles:
                part = s_buf[slot, k : k + TILE, lanes].reshape(TILE // 8, 8, step)
                part = jnp.max(part, 0)
                top = part if top is None else jnp.maximum(top, part)
            top = jnp.max(top, 0, keepdims=True)
            if state_in is not None:
                old = state_in[TOP_ROW : TOP_ROW + 1, c * wide + j : c * wide + j + step]
                top = jnp.maximum(top, old)
                factors.append(jnp.exp2((old - top) * TO_EXP2))
            for k, lanes in tiles:
                weights = jnp.exp2((s_buf[slot, k : k + TILE, lanes] - top) * TO_EXP2)
                p_buf[slot, k : k + TILE, lanes] = weights.astype(jnp.bfloat16)
            tops.append(top)
        top = jnp.concatenate(tops, 1)
        return top, (jnp.concatenate(factors, 1) if factors else None)

    def sum_up(c, top, factor):
        lanes = slice(c * wide, (c + 1) * wide)
        summed = dot(value_ext[c // per_group], p_buf[c % slots], ((1,), (0,)))[:TOP_ROW]
        if factor is not None:
            summed = summed + state_in[0:TOP_ROW, lanes] * factor
        if out_ref is None:
            state_out[0:TOP_ROW, lanes] = summed
            state_out[TOP_ROW : TOP_ROW + 1, lanes] = top
        else:
            finish(summed, top, c, heads, out_ref, log_ref)

    held = {}
    for t in range(chunks + 2):
        if t < chunks:
            score(t)
        if 0 <= t - 1 < chunks:
            held[t - 1] = weigh(t - 1)
        if 0 <= t - 2 < chunks:
            sum_up(t - 2, *held.pop(t - 2))


def finish(summed, top, c, heads, out_ref, log_ref):
    total = summed[HD : HD + 1]
    result = summed[:HD] * (1.0 / total)
    logs = top * SCALE + jnp.log(total)
    first = c * heads
    for h in range(heads):
        lanes = slice(h * HD, (h + 1) * HD)
        out_ref[:, (first + h) * HD : (first + h + 1) * HD] = result[:, lanes].T.astype(
            out_ref.dtype
        )
    log_ref[first : first + heads, :] = jnp.concatenate(
        [logs[:, h * HD : (h + 1) * HD] for h in range(heads)], 0
    )


def lane_row(rows):
    lane = lax.broadcasted_iota(jnp.int32, (rows, HD), 1)
    row = lax.broadcasted_iota(jnp.int32, (rows, HD), 0)
    return lane, row


def lowest_of(mark_ref):
    return jnp.max(mark_ref[...]).astype(jnp.int32)


def near_kernel(axis, mark_in, q_ref, own, other, state_out, mark, s_buf, p_buf):
    me = lax.axis_index(axis)
    rows = own.shape[0]
    lowest = lowest_of(mark_in)
    mark[...] = mark_in[...]
    lane, row = lane_row(rows)
    first_seen = jnp.where((me & 1) == 1, lowest - (me - 1) * rows, rows)
    other_flags = jnp.where((lane == 0) & (row < first_seen), 1.0, 0.0)
    own_flags = jnp.where((lane == row) & (row > 0), 1.0, 0.0)
    flags = jnp.concatenate([other_flags, own_flags], 0).astype(jnp.bfloat16)
    row_flags = jnp.where((lane == 0) | (lane > row), HIDDEN, 0.0).astype(jnp.bfloat16)
    run_chunks(
        q_ref, [other, own], flags, row_flags, None, state_out, s_buf, p_buf, None, None
    )


def far_kernel(axis, pieces, last, mark_in, q_ref, *refs):
    me = lax.axis_index(axis)
    count = len(pieces)
    blocks, state_in = refs[:count], refs[count]
    if last:
        state_out, (out_ref, log_ref, s_buf, p_buf) = None, refs[count + 1 :]
    else:
        (state_out, mark, s_buf, p_buf), out_ref, log_ref = refs[count + 1 :], None, None
        mark[...] = mark_in[...]
    rows = blocks[0].shape[0]
    lowest = lowest_of(mark_in)
    starts = [((me ^ side) - distance) * rows for distance, side in pieces]
    needed = functools.reduce(jnp.logical_or, [s + rows > lowest for s in starts])

    @pl.when(needed)
    def _():
        lane, row = lane_row(rows)
        flags = jnp.concatenate(
            [jnp.where((lane == 0) & (row + s < lowest), 1.0, 0.0) for s in starts], 0
        ).astype(jnp.bfloat16)
        row_flags = jnp.where(lane == 0, HIDDEN, 0.0).astype(jnp.bfloat16)
        run_chunks(
            q_ref, blocks, flags, row_flags, state_in, state_out, s_buf, p_buf, out_ref, log_ref
        )

    @pl.when(jnp.logical_not(needed))
    def _():
        if last:
            wide = s_buf.shape[2]
            for c in range(q_ref.shape[1] // wide):
                lanes = slice(c * wide, (c + 1) * wide)
                top = state_in[TOP_ROW : TOP_ROW + 1, lanes]
                finish(state_in[0:TOP_ROW, lanes], top, c, wide // HD, out_ref, log_ref)
        else:
            state_out[...] = state_in[...]


def attend(kernel, mark, queries, blocks, state, last):
    rows, width = queries.shape
    heads = width // HD
    groups = blocks[0].shape[1] // (2 * HD)
    wide = HD * math.gcd(heads // groups, 4)
    keys = len(blocks) * rows
    operands = [mark, queries, *blocks]
    aliases = {}
    if state is not None:
        if not last:
            aliases = {len(operands): 0}
        operands.append(state)
    if last:
        out_shape = [
            jax.ShapeDtypeStruct((rows, width), jnp.bfloat16),
            jax.ShapeDtypeStruct((heads, rows), jnp.float32),
        ]
    else:
        out_shape = [
            jax.ShapeDtypeStruct((STATE_ROWS, width), jnp.float32),
            jax.ShapeDtypeStruct(MARK, jnp.float32),
        ]
    return pl.pallas_call(
        kernel,
        in_specs=[VMEM] * len(operands),
        out_specs=[VMEM] * len(out_shape),
        out_shape=out_shape,
        scratch_shapes=[
            pltpu.VMEM((2, keys, wide), jnp.float32),
            pltpu.VMEM((2, keys, wide), jnp.bfloat16),
        ],
        input_output_aliases=aliases,
        cost_estimate=pl.CostEstimate(
            flops=4 * keys * rows * width,
            bytes_accessed=rows * width * 2,
            transcendentals=keys * rows * heads,
        ),
        compiler_params=pltpu.CompilerParams(vmem_limit_bytes=12 << 20),
    )(*operands)


def fetch_kernel(axis, k_hbm, v_hbm, win_hbm, q_hbm, own_ref, mark_ref, q_ref, win_ref, sems):
    rows, width = k_hbm.shape
    copies = [
        pltpu.make_async_copy(k_hbm, own_ref.at[:, pl.ds(0, width)], sems.at[0]),
        pltpu.make_async_copy(v_hbm, own_ref.at[:, pl.ds(width, width)], sems.at[1]),
        pltpu.make_async_copy(win_hbm, win_ref, sems.at[2]),
        pltpu.make_async_copy(q_hbm, q_ref, sems.at[3]),
    ]
    for copy in copies:
        copy.start()
    for copy in copies:
        copy.wait()
    me = lax.axis_index(axis)
    lowest = jnp.maximum(me * rows - win_ref[me], 0)
    mark_ref[...] = jnp.full(mark_ref.shape, lowest.astype(jnp.float32))


def fetched(axis, queries, keys, values, windows):
    rows, width = keys.shape
    sources = [
        pltpu.with_memory_space_constraint(x, pltpu.HBM) for x in (keys, values, windows, queries)
    ]
    return pl.pallas_call(
        functools.partial(fetch_kernel, axis),
        in_specs=[HBM] * 4,
        out_specs=[VMEM] * 3,
        out_shape=[
            jax.ShapeDtypeStruct((rows, 2 * width), keys.dtype),
            jax.ShapeDtypeStruct(MARK, jnp.float32),
            jax.ShapeDtypeStruct(queries.shape, queries.dtype),
        ],
        scratch_shapes=[
            pltpu.SMEM(windows.shape, windows.dtype),
            pltpu.SemaphoreType.DMA((4,)),
        ],
        compiler_params=SMALL,
    )(*sources)


def tied(block, earlier):
    def kernel(block_ref, earlier_ref, out_ref):
        pass

    return pl.pallas_call(
        kernel,
        in_specs=[VMEM, VMEM],
        out_specs=VMEM,
        out_shape=jax.ShapeDtypeStruct(block.shape, block.dtype),
        input_output_aliases={0: 0},
        compiler_params=SMALL,
    )(block, earlier)


def on_device(queries, keys, values, windows):
    axis = "section"
    reach = lax.axis_size(axis) // 2
    own, mark, queries = fetched(axis, queries, keys, values, windows)
    other = swapped(own, axis)
    held = {d: shifted(own, axis, d) for d in (4, 2)}
    state, mark = attend(
        functools.partial(near_kernel, axis), mark, queries, [own, other], None, False
    )
    for first in range(2, reach + 1, 4):
        distances = [d for d in (first + 2, first) if d <= reach]
        last = first + 4 > reach
        mine, theirs = {}, {}
        for d in distances:
            held[d] = tied(held[d], mark)
            if d + 4 <= reach:
                held[d + 4] = shifted(held[d], axis, 4, d)
            mine[d, 0] = held[d]
            theirs[d, 1] = swapped(held[d], axis)
        for blocks in (mine, theirs) if last else ({**mine, **theirs},):
            final = last and blocks is theirs
            result = attend(
                functools.partial(far_kernel, axis, list(blocks), final),
                mark,
                queries,
                list(blocks.values()),
                state,
                final,
            )
            state, mark = result
    return result[0], result[1].T


def solution(mesh):
    placed = (
        P(("groups", "section"), None),
        P(("groups", "section"), None),
        P(("groups", "section"), None),
        P("groups"),
    )
    return jax.shard_map(
        on_device,
        mesh=mesh,
        in_specs=placed,
        out_specs=(P(("groups", "section"), None), P(("groups", "section"), None)),
        check_vma=False,
    )
```

```python
import functools
import math

import jax
import jax.numpy as jnp
from jax import lax
from jax.experimental import pallas as pl
from jax.experimental.pallas import tpu as pltpu
from jax.sharding import PartitionSpec as P

HD = 128
SCALE = HD ** (-0.5)
TO_EXP2 = SCALE * math.log2(math.e)
HIDDEN = -1e30
SUM_ROWS = 8
STATE_ROWS = HD + 2 * SUM_ROWS
TOP_ROW = HD + SUM_ROWS
TILE = 64
VMEM = pl.BlockSpec(memory_space=pltpu.VMEM)
SMALL = pltpu.CompilerParams(vmem_limit_bytes=1 << 20)
HBM = pl.BlockSpec(memory_space=pltpu.HBM)
MARK = (8, HD)


def shifted(block, axis, distance):
    size = lax.axis_size(axis)
    return lax.ppermute(block, axis, [(i, (i + distance) % size) for i in range(size)])


def swapped(block, axis):
    return lax.ppermute(block, axis, [(i ^ 1, i) for i in range(lax.axis_size(axis))])


def dot(left, right, dims):
    return lax.dot_general(left, right, (dims, ((), ())), preferred_element_type=jnp.float32)


def run_chunks(q_ref, blocks, flags, row_flags, state_in, state_out, s_buf, p_buf, out_ref, log_ref):
    rows, width = q_ref.shape
    groups = blocks[0].shape[1] // (2 * HD)
    slots, keys, wide = s_buf.shape
    heads = wide // HD
    chunks = width // wide
    per_group = chunks // groups
    row_part = jnp.concatenate([row_flags] * heads, 0)
    ones = jnp.ones((2 * SUM_ROWS, keys), jnp.bfloat16)
    key_ext, value_ext = [], []
    for g in range(groups):
        key_rows = jnp.concatenate([b[:, g * HD : (g + 1) * HD] for b in blocks], 0)
        value_rows = jnp.concatenate(
            [b[:, (groups + g) * HD : (groups + g + 1) * HD] for b in blocks], 0
        )
        key_ext.append(jnp.concatenate([key_rows, flags], 1))
        value_ext.append(jnp.concatenate([value_rows.T, ones], 0))

    def score(c):
        parts = [q_ref[:, c * wide + h * HD : c * wide + (h + 1) * HD] for h in range(heads)]
        query_rows = jnp.concatenate([jnp.concatenate(parts, 0), row_part], 1)
        s_buf[c % slots] = dot(key_ext[c // per_group], query_rows, ((1,), (1,)))

    def weigh(c):
        slot, step = c % slots, min(2 * HD, wide)
        tops, factors = [], []
        for j in range(0, wide, step):
            tiles = [
                (k, slice(j, j + step)) for k in range(0, keys, TILE)
            ]
            top = None
            for k, lanes in tiles:
                part = s_buf[slot, k : k + TILE, lanes].reshape(TILE // 8, 8, step)
                part = jnp.max(part, 0)
                top = part if top is None else jnp.maximum(top, part)
            top = jnp.max(top, 0, keepdims=True)
            if state_in is not None:
                old = state_in[TOP_ROW : TOP_ROW + 1, c * wide + j : c * wide + j + step]
                top = jnp.maximum(top, old)
                factors.append(jnp.exp2((old - top) * TO_EXP2))
            for k, lanes in tiles:
                weights = jnp.exp2((s_buf[slot, k : k + TILE, lanes] - top) * TO_EXP2)
                p_buf[slot, k : k + TILE, lanes] = weights.astype(jnp.bfloat16)
            tops.append(top)
        top = jnp.concatenate(tops, 1)
        return top, (jnp.concatenate(factors, 1) if factors else None)

    def sum_up(c, top, factor):
        lanes = slice(c * wide, (c + 1) * wide)
        summed = dot(value_ext[c // per_group], p_buf[c % slots], ((1,), (0,)))[:TOP_ROW]
        if factor is not None:
            summed = summed + state_in[0:TOP_ROW, lanes] * factor
        if out_ref is None:
            state_out[0:TOP_ROW, lanes] = summed
            state_out[TOP_ROW : TOP_ROW + 1, lanes] = top
        else:
            finish(summed, top, c, heads, out_ref, log_ref)

    held = {}
    for t in range(chunks + 2):
        if t < chunks:
            score(t)
        if 0 <= t - 1 < chunks:
            held[t - 1] = weigh(t - 1)
        if 0 <= t - 2 < chunks:
            sum_up(t - 2, *held.pop(t - 2))


def finish(summed, top, c, heads, out_ref, log_ref):
    total = summed[HD : HD + 1]
    result = summed[:HD] * (1.0 / total)
    logs = top * SCALE + jnp.log(total)
    first = c * heads
    for h in range(heads):
        lanes = slice(h * HD, (h + 1) * HD)
        out_ref[:, (first + h) * HD : (first + h + 1) * HD] = result[:, lanes].T.astype(
            out_ref.dtype
        )
    log_ref[first : first + heads, :] = jnp.concatenate(
        [logs[:, h * HD : (h + 1) * HD] for h in range(heads)], 0
    )


def lane_row(rows):
    lane = lax.broadcasted_iota(jnp.int32, (rows, HD), 1)
    row = lax.broadcasted_iota(jnp.int32, (rows, HD), 0)
    return lane, row


def lowest_of(mark_ref):
    return jnp.max(mark_ref[...]).astype(jnp.int32)


def near_kernel(axis, mark_in, q_ref, own, other, state_out, mark, s_buf, p_buf):
    me = lax.axis_index(axis)
    rows = own.shape[0]
    lowest = lowest_of(mark_in)
    mark[...] = mark_in[...]
    lane, row = lane_row(rows)
    first_seen = jnp.where((me & 1) == 1, lowest - (me - 1) * rows, rows)
    other_flags = jnp.where((lane == 0) & (row < first_seen), 1.0, 0.0)
    own_flags = jnp.where((lane == row) & (row > 0), 1.0, 0.0)
    flags = jnp.concatenate([other_flags, own_flags], 0).astype(jnp.bfloat16)
    row_flags = jnp.where((lane == 0) | (lane > row), HIDDEN, 0.0).astype(jnp.bfloat16)
    run_chunks(
        q_ref, [other, own], flags, row_flags, None, state_out, s_buf, p_buf, None, None
    )


def far_kernel(axis, pieces, last, mark_in, q_ref, *refs):
    me = lax.axis_index(axis)
    count = len(pieces)
    blocks, state_in = refs[:count], refs[count]
    if last:
        state_out, (out_ref, log_ref, s_buf, p_buf) = None, refs[count + 1 :]
    else:
        (state_out, mark, s_buf, p_buf), out_ref, log_ref = refs[count + 1 :], None, None
        mark[...] = mark_in[...]
    rows = blocks[0].shape[0]
    lowest = lowest_of(mark_in)
    starts = [((me ^ side) - distance) * rows for distance, side in pieces]
    needed = functools.reduce(jnp.logical_or, [s + rows > lowest for s in starts])

    @pl.when(needed)
    def _():
        lane, row = lane_row(rows)
        flags = jnp.concatenate(
            [jnp.where((lane == 0) & (row + s < lowest), 1.0, 0.0) for s in starts], 0
        ).astype(jnp.bfloat16)
        row_flags = jnp.where(lane == 0, HIDDEN, 0.0).astype(jnp.bfloat16)
        run_chunks(
            q_ref, blocks, flags, row_flags, state_in, state_out, s_buf, p_buf, out_ref, log_ref
        )

    @pl.when(jnp.logical_not(needed))
    def _():
        if last:
            wide = s_buf.shape[2]
            for c in range(q_ref.shape[1] // wide):
                lanes = slice(c * wide, (c + 1) * wide)
                top = state_in[TOP_ROW : TOP_ROW + 1, lanes]
                finish(state_in[0:TOP_ROW, lanes], top, c, wide // HD, out_ref, log_ref)
        else:
            state_out[...] = state_in[...]


def attend(kernel, mark, queries, blocks, state, last):
    rows, width = queries.shape
    heads = width // HD
    groups = blocks[0].shape[1] // (2 * HD)
    wide = HD * math.gcd(heads // groups, 4)
    keys = len(blocks) * rows
    operands = [mark, queries, *blocks]
    aliases = {}
    if state is not None:
        if not last:
            aliases = {len(operands): 0}
        operands.append(state)
    if last:
        out_shape = [
            jax.ShapeDtypeStruct((rows, width), jnp.bfloat16),
            jax.ShapeDtypeStruct((heads, rows), jnp.float32),
        ]
    else:
        out_shape = [
            jax.ShapeDtypeStruct((STATE_ROWS, width), jnp.float32),
            jax.ShapeDtypeStruct(MARK, jnp.float32),
        ]
    return pl.pallas_call(
        kernel,
        in_specs=[VMEM] * len(operands),
        out_specs=[VMEM] * len(out_shape),
        out_shape=out_shape,
        scratch_shapes=[
            pltpu.VMEM((2, keys, wide), jnp.float32),
            pltpu.VMEM((2, keys, wide), jnp.bfloat16),
        ],
        input_output_aliases=aliases,
        cost_estimate=pl.CostEstimate(
            flops=4 * keys * rows * width,
            bytes_accessed=rows * width * 2,
            transcendentals=keys * rows * heads,
        ),
        compiler_params=pltpu.CompilerParams(vmem_limit_bytes=12 << 20),
    )(*operands)


def fetch_kernel(axis, k_hbm, v_hbm, win_hbm, q_hbm, own_ref, mark_ref, q_ref, win_ref, sems):
    rows, width = k_hbm.shape
    copies = [
        pltpu.make_async_copy(k_hbm, own_ref.at[:, pl.ds(0, width)], sems.at[0]),
        pltpu.make_async_copy(v_hbm, own_ref.at[:, pl.ds(width, width)], sems.at[1]),
        pltpu.make_async_copy(win_hbm, win_ref, sems.at[2]),
        pltpu.make_async_copy(q_hbm, q_ref, sems.at[3]),
    ]
    for copy in copies:
        copy.start()
    for copy in copies:
        copy.wait()
    me = lax.axis_index(axis)
    lowest = jnp.maximum(me * rows - win_ref[me], 0)
    mark_ref[...] = jnp.full(mark_ref.shape, lowest.astype(jnp.float32))


def fetched(axis, queries, keys, values, windows):
    rows, width = keys.shape
    sources = [
        pltpu.with_memory_space_constraint(x, pltpu.HBM) for x in (keys, values, windows, queries)
    ]
    return pl.pallas_call(
        functools.partial(fetch_kernel, axis),
        in_specs=[HBM] * 4,
        out_specs=[VMEM] * 3,
        out_shape=[
            jax.ShapeDtypeStruct((rows, 2 * width), keys.dtype),
            jax.ShapeDtypeStruct(MARK, jnp.float32),
            jax.ShapeDtypeStruct(queries.shape, queries.dtype),
        ],
        scratch_shapes=[
            pltpu.SMEM(windows.shape, windows.dtype),
            pltpu.SemaphoreType.DMA((4,)),
        ],
        compiler_params=SMALL,
    )(*sources)


def tied(block, earlier):
    def kernel(block_ref, earlier_ref, out_ref):
        pass

    return pl.pallas_call(
        kernel,
        in_specs=[VMEM, VMEM],
        out_specs=VMEM,
        out_shape=jax.ShapeDtypeStruct(block.shape, block.dtype),
        input_output_aliases={0: 0},
        compiler_params=SMALL,
    )(block, earlier)


def on_device(queries, keys, values, windows):
    axis = "section"
    reach = lax.axis_size(axis) // 2
    own, mark, queries = fetched(axis, queries, keys, values, windows)
    other = swapped(own, axis)
    held = {d: shifted(own, axis, d) for d in (4, 2)}
    state, mark = attend(
        functools.partial(near_kernel, axis), mark, queries, [own, other], None, False
    )
    order = [d for first in range(2, reach + 1, 4) for d in (first + 2, first) if d <= reach]
    early = max(len(order) - 2, 0)
    groups = [[d] for d in order[:early]] + [order[early:]]
    for group in groups:
        last = group is groups[-1]
        blocks = {}
        for d in group:
            held[d] = tied(held[d], mark)
            if d + 4 <= reach:
                held[d + 4] = shifted(held[d], axis, 4)
            blocks[d, 0] = held[d]
            blocks[d, 1] = swapped(held[d], axis)
        result = attend(
            functools.partial(far_kernel, axis, list(blocks), last),
            mark,
            queries,
            list(blocks.values()),
            state,
            last,
        )
        state, mark = result
    return result[0], result[1].T


def solution(mesh):
    placed = (
        P(("groups", "section"), None),
        P(("groups", "section"), None),
        P(("groups", "section"), None),
        P("groups"),
    )
    return jax.shard_map(
        on_device,
        mesh=mesh,
        in_specs=placed,
        out_specs=(P(("groups", "section"), None), P(("groups", "section"), None)),
        check_vma=False,
    )
```

```python
import functools
import math

import jax
import jax.numpy as jnp
from jax import lax
from jax.experimental import pallas as pl
from jax.experimental.pallas import tpu as pltpu
from jax.sharding import PartitionSpec as P

HD = 128
SCALE = HD ** (-0.5)
TO_EXP2 = SCALE * math.log2(math.e)
HIDDEN = -1e30
SUM_ROWS = 8
STATE_ROWS = HD + 2 * SUM_ROWS
TOP_ROW = HD + SUM_ROWS
TILE = 64
VMEM = pl.BlockSpec(memory_space=pltpu.VMEM)
SMALL = pltpu.CompilerParams(vmem_limit_bytes=1 << 20)
HBM = pl.BlockSpec(memory_space=pltpu.HBM)
MARK = (8, HD)


def shifted(block, axis, distance):
    size = lax.axis_size(axis)
    return lax.ppermute(block, axis, [(i, (i + distance) % size) for i in range(size)])


def swapped(block, axis):
    return lax.ppermute(block, axis, [(i ^ 1, i) for i in range(lax.axis_size(axis))])


def dot(left, right, dims):
    return lax.dot_general(left, right, (dims, ((), ())), preferred_element_type=jnp.float32)


def run_chunks(q_ref, blocks, flags, row_flags, state_in, state_out, s_buf, p_buf, outs):
    rows, width = q_ref.shape
    groups = blocks[0].shape[1] // (2 * HD)
    slots, keys, wide = s_buf.shape
    heads = wide // HD
    chunks = width // wide
    per_group = chunks // groups
    row_part = jnp.concatenate([row_flags] * heads, 0)
    ones = jnp.ones((2 * SUM_ROWS, keys), jnp.bfloat16)
    key_ext, value_ext = [], []
    for g in range(groups):
        key_rows = jnp.concatenate([b[:, g * HD : (g + 1) * HD] for b in blocks], 0)
        value_rows = jnp.concatenate(
            [b[:, (groups + g) * HD : (groups + g + 1) * HD] for b in blocks], 0
        )
        key_ext.append(jnp.concatenate([key_rows, flags], 1))
        value_ext.append(jnp.concatenate([value_rows.T, ones], 0))

    def score(c):
        parts = [q_ref[:, c * wide + h * HD : c * wide + (h + 1) * HD] for h in range(heads)]
        query_rows = jnp.concatenate([jnp.concatenate(parts, 0), row_part], 1)
        s_buf[c % slots] = dot(key_ext[c // per_group], query_rows, ((1,), (1,)))

    def weigh(c):
        slot, step = c % slots, min(2 * HD, wide)
        tops, factors = [], []
        for j in range(0, wide, step):
            tiles = [
                (k, slice(j, j + step)) for k in range(0, keys, TILE)
            ]
            top = None
            for k, lanes in tiles:
                part = s_buf[slot, k : k + TILE, lanes].reshape(TILE // 8, 8, step)
                part = jnp.max(part, 0)
                top = part if top is None else jnp.maximum(top, part)
            top = jnp.max(top, 0, keepdims=True)
            if state_in is not None:
                old = state_in[TOP_ROW : TOP_ROW + 1, c * wide + j : c * wide + j + step]
                top = jnp.maximum(top, old)
                factors.append(jnp.exp2((old - top) * TO_EXP2))
            for k, lanes in tiles:
                weights = jnp.exp2((s_buf[slot, k : k + TILE, lanes] - top) * TO_EXP2)
                p_buf[slot, k : k + TILE, lanes] = weights.astype(jnp.bfloat16)
            tops.append(top)
        top = jnp.concatenate(tops, 1)
        return top, (jnp.concatenate(factors, 1) if factors else None)

    def sum_up(c, top, factor):
        lanes = slice(c * wide, (c + 1) * wide)
        summed = dot(value_ext[c // per_group], p_buf[c % slots], ((1,), (0,)))[:TOP_ROW]
        if factor is not None:
            summed = summed + state_in[0:TOP_ROW, lanes] * factor
        if outs is None:
            state_out[0:TOP_ROW, lanes] = summed
            state_out[TOP_ROW : TOP_ROW + 1, lanes] = top
        else:
            finish(summed, top, c, heads, *outs)

    held = {}
    for t in range(chunks + 2):
        if t < chunks:
            score(t)
        if 0 <= t - 1 < chunks:
            held[t - 1] = weigh(t - 1)
        if 0 <= t - 2 < chunks:
            sum_up(t - 2, *held.pop(t - 2))


def write_back(c, wide, out_hbm, out_buf, sems):
    lanes = pl.ds(c * wide, wide)
    return pltpu.make_async_copy(out_buf.at[:, lanes], out_hbm.at[:, lanes], sems.at[c])


def finish(summed, top, c, heads, out_hbm, log_ref, out_buf, sems):
    total = summed[HD : HD + 1]
    result = summed[:HD] * (1.0 / total)
    logs = top * SCALE + jnp.log(total)
    first = c * heads
    for h in range(heads):
        lanes = slice(h * HD, (h + 1) * HD)
        out_buf[:, (first + h) * HD : (first + h + 1) * HD] = result[:, lanes].T.astype(
            out_buf.dtype
        )
    write_back(c, heads * HD, out_hbm, out_buf, sems).start()
    log_ref[first : first + heads, :] = jnp.concatenate(
        [logs[:, h * HD : (h + 1) * HD] for h in range(heads)], 0
    )


def lane_row(rows):
    lane = lax.broadcasted_iota(jnp.int32, (rows, HD), 1)
    row = lax.broadcasted_iota(jnp.int32, (rows, HD), 0)
    return lane, row


def lowest_of(mark_ref):
    return jnp.max(mark_ref[...]).astype(jnp.int32)


def near_kernel(axis, mark_in, q_ref, own, other, state_out, mark, s_buf, p_buf):
    me = lax.axis_index(axis)
    rows = own.shape[0]
    lowest = lowest_of(mark_in)
    mark[...] = mark_in[...]
    lane, row = lane_row(rows)
    first_seen = jnp.where((me & 1) == 1, lowest - (me - 1) * rows, rows)
    other_flags = jnp.where((lane == 0) & (row < first_seen), 1.0, 0.0)
    own_flags = jnp.where((lane == row) & (row > 0), 1.0, 0.0)
    flags = jnp.concatenate([other_flags, own_flags], 0).astype(jnp.bfloat16)
    row_flags = jnp.where((lane == 0) | (lane > row), HIDDEN, 0.0).astype(jnp.bfloat16)
    run_chunks(
        q_ref, [other, own], flags, row_flags, None, state_out, s_buf, p_buf, None
    )


def far_kernel(axis, distances, last, mark_in, q_ref, *refs):
    me = lax.axis_index(axis)
    count = 2 * len(distances)
    blocks, state_in = refs[:count], refs[count]
    if last:
        state_out, (out_hbm, log_ref, s_buf, p_buf, out_buf, sems) = None, refs[count + 1 :]
        outs = (out_hbm, log_ref, out_buf, sems)
    else:
        (state_out, mark, s_buf, p_buf), outs = refs[count + 1 :], None
        mark[...] = mark_in[...]
    rows = blocks[0].shape[0]
    lowest = lowest_of(mark_in)
    starts = [(who - d) * rows for d in distances for who in (me, me ^ 1)]
    needed = functools.reduce(jnp.logical_or, [s + rows > lowest for s in starts])

    @pl.when(needed)
    def _():
        lane, row = lane_row(rows)
        flags = jnp.concatenate(
            [jnp.where((lane == 0) & (row + s < lowest), 1.0, 0.0) for s in starts], 0
        ).astype(jnp.bfloat16)
        row_flags = jnp.where(lane == 0, HIDDEN, 0.0).astype(jnp.bfloat16)
        run_chunks(
            q_ref, blocks, flags, row_flags, state_in, state_out, s_buf, p_buf, outs
        )

    wide = s_buf.shape[2]
    chunks = q_ref.shape[1] // wide

    @pl.when(jnp.logical_not(needed))
    def _():
        if last:
            for c in range(chunks):
                lanes = slice(c * wide, (c + 1) * wide)
                top = state_in[TOP_ROW : TOP_ROW + 1, lanes]
                finish(state_in[0:TOP_ROW, lanes], top, c, wide // HD, *outs)
        else:
            state_out[...] = state_in[...]

    if last:
        for c in range(chunks):
            write_back(c, wide, out_hbm, out_buf, sems).wait()


def attend(kernel, mark, queries, blocks, state, last):
    rows, width = queries.shape
    heads = width // HD
    groups = blocks[0].shape[1] // (2 * HD)
    wide = HD * math.gcd(heads // groups, 4)
    keys = len(blocks) * rows
    operands = [mark, queries, *blocks]
    aliases = {}
    if state is not None:
        if not last:
            aliases = {len(operands): 0}
        operands.append(state)
    if last:
        out_shape = [
            jax.ShapeDtypeStruct((rows, width), jnp.bfloat16),
            jax.ShapeDtypeStruct((heads, rows), jnp.float32),
        ]
    else:
        out_shape = [
            jax.ShapeDtypeStruct((STATE_ROWS, width), jnp.float32),
            jax.ShapeDtypeStruct(MARK, jnp.float32),
        ]
    scratch = [
        pltpu.VMEM((2, keys, wide), jnp.float32),
        pltpu.VMEM((2, keys, wide), jnp.bfloat16),
    ]
    if last:
        scratch += [
            pltpu.VMEM((rows, width), jnp.bfloat16),
            pltpu.SemaphoreType.DMA((width // wide,)),
        ]
    return pl.pallas_call(
        kernel,
        in_specs=[VMEM] * len(operands),
        out_specs=[HBM, VMEM] if last else [VMEM] * 2,
        out_shape=out_shape,
        scratch_shapes=scratch,
        input_output_aliases=aliases,
        cost_estimate=pl.CostEstimate(
            flops=4 * keys * rows * width,
            bytes_accessed=rows * width * 2,
            transcendentals=keys * rows * heads,
        ),
        compiler_params=pltpu.CompilerParams(vmem_limit_bytes=12 << 20),
    )(*operands)


def fetch_kernel(axis, k_hbm, v_hbm, win_hbm, q_hbm, own_ref, mark_ref, q_ref, win_ref, sems):
    rows, width = k_hbm.shape
    copies = [
        pltpu.make_async_copy(k_hbm, own_ref.at[:, pl.ds(0, width)], sems.at[0]),
        pltpu.make_async_copy(v_hbm, own_ref.at[:, pl.ds(width, width)], sems.at[1]),
        pltpu.make_async_copy(win_hbm, win_ref, sems.at[2]),
        pltpu.make_async_copy(q_hbm, q_ref, sems.at[3]),
    ]
    for copy in copies:
        copy.start()
    for copy in copies:
        copy.wait()
    me = lax.axis_index(axis)
    lowest = jnp.maximum(me * rows - win_ref[me], 0)
    mark_ref[...] = jnp.full(mark_ref.shape, lowest.astype(jnp.float32))


def fetched(axis, queries, keys, values, windows):
    rows, width = keys.shape
    sources = [
        pltpu.with_memory_space_constraint(x, pltpu.HBM) for x in (keys, values, windows, queries)
    ]
    return pl.pallas_call(
        functools.partial(fetch_kernel, axis),
        in_specs=[HBM] * 4,
        out_specs=[VMEM] * 3,
        out_shape=[
            jax.ShapeDtypeStruct((rows, 2 * width), keys.dtype),
            jax.ShapeDtypeStruct(MARK, jnp.float32),
            jax.ShapeDtypeStruct(queries.shape, queries.dtype),
        ],
        scratch_shapes=[
            pltpu.SMEM(windows.shape, windows.dtype),
            pltpu.SemaphoreType.DMA((4,)),
        ],
        compiler_params=SMALL,
    )(*sources)


def tied(block, earlier):
    def kernel(block_ref, earlier_ref, out_ref):
        pass

    return pl.pallas_call(
        kernel,
        in_specs=[VMEM, VMEM],
        out_specs=VMEM,
        out_shape=jax.ShapeDtypeStruct(block.shape, block.dtype),
        input_output_aliases={0: 0},
        compiler_params=SMALL,
    )(block, earlier)


def on_device(queries, keys, values, windows):
    axis = "section"
    reach = lax.axis_size(axis) // 2
    own, mark, queries = fetched(axis, queries, keys, values, windows)
    other = swapped(own, axis)
    held = {4: shifted(own, axis, 4), 2: shifted(own, axis, 2)}
    state, mark = attend(
        functools.partial(near_kernel, axis), mark, queries, [own, other], None, False
    )
    for first in range(2, reach + 1, 4):
        distances = [d for d in (first, first + 2) if d <= reach]
        last = first + 4 > reach
        blocks = []
        for d in distances:
            held[d] = tied(held[d], mark)
            if d + 4 <= reach:
                held[d + 4] = shifted(held[d], axis, 4)
            blocks += [held[d], swapped(held[d], axis)]
        result = attend(
            functools.partial(far_kernel, axis, distances, last),
            mark,
            queries,
            blocks,
            state,
            last,
        )
        state, mark = result
    return result[0], result[1].T


def solution(mesh):
    placed = (
        P(("groups", "section"), None),
        P(("groups", "section"), None),
        P(("groups", "section"), None),
        P("groups"),
    )
    return jax.shard_map(
        on_device,
        mesh=mesh,
        in_specs=placed,
        out_specs=(P(("groups", "section"), None), P(("groups", "section"), None)),
        check_vma=False,
    )
```

```python
import functools
import math

import jax
import jax.numpy as jnp
from jax import lax
from jax.experimental import pallas as pl
from jax.experimental.pallas import tpu as pltpu
from jax.sharding import PartitionSpec as P

HD = 128
SCALE = HD ** (-0.5)
TO_EXP2 = SCALE * math.log2(math.e)
HIDDEN = -1e30
SUM_ROWS = 8
STATE_ROWS = HD + 2 * SUM_ROWS
TOP_ROW = HD + SUM_ROWS
TILE = 64
VMEM = pl.BlockSpec(memory_space=pltpu.VMEM)
SMALL = pltpu.CompilerParams(vmem_limit_bytes=1 << 20)
HBM = pl.BlockSpec(memory_space=pltpu.HBM)
MARK = (8, HD)


def first_reach(core, turn):
    return 4 - 2 * (core ^ turn)


def shifted(block, axis, distances):
    size = lax.axis_size(axis)
    return lax.ppermute(block, axis, [(i, (i + distances[i % 2]) % size) for i in range(size)])


def swapped(block, axis):
    return lax.ppermute(block, axis, [(i ^ 1, i) for i in range(lax.axis_size(axis))])


def dot(left, right, dims):
    return lax.dot_general(left, right, (dims, ((), ())), preferred_element_type=jnp.float32)


def run_chunks(q_ref, blocks, flags, row_flags, state_in, state_out, s_buf, p_buf, out_ref, log_ref):
    rows, width = q_ref.shape
    groups = blocks[0].shape[1] // (2 * HD)
    slots, keys, wide = s_buf.shape
    heads = wide // HD
    chunks = width // wide
    per_group = chunks // groups
    row_part = jnp.concatenate([row_flags] * heads, 0)
    ones = jnp.ones((2 * SUM_ROWS, keys), jnp.bfloat16)
    key_ext, value_ext = [], []
    for g in range(groups):
        key_rows = jnp.concatenate([b[:, g * HD : (g + 1) * HD] for b in blocks], 0)
        value_rows = jnp.concatenate(
            [b[:, (groups + g) * HD : (groups + g + 1) * HD] for b in blocks], 0
        )
        key_ext.append(jnp.concatenate([key_rows, flags], 1))
        value_ext.append(jnp.concatenate([value_rows.T, ones], 0))

    def score(c):
        parts = [q_ref[:, c * wide + h * HD : c * wide + (h + 1) * HD] for h in range(heads)]
        query_rows = jnp.concatenate([jnp.concatenate(parts, 0), row_part], 1)
        s_buf[c % slots] = dot(key_ext[c // per_group], query_rows, ((1,), (1,)))

    def weigh(c):
        slot, step = c % slots, min(2 * HD, wide)
        tops, factors = [], []
        for j in range(0, wide, step):
            tiles = [
                (k, slice(j, j + step)) for k in range(0, keys, TILE)
            ]
            top = None
            for k, lanes in tiles:
                part = s_buf[slot, k : k + TILE, lanes].reshape(TILE // 8, 8, step)
                part = jnp.max(part, 0)
                top = part if top is None else jnp.maximum(top, part)
            top = jnp.max(top, 0, keepdims=True)
            if state_in is not None:
                old = state_in[TOP_ROW : TOP_ROW + 1, c * wide + j : c * wide + j + step]
                top = jnp.maximum(top, old)
                factors.append(jnp.exp2((old - top) * TO_EXP2))
            for k, lanes in tiles:
                weights = jnp.exp2((s_buf[slot, k : k + TILE, lanes] - top) * TO_EXP2)
                p_buf[slot, k : k + TILE, lanes] = weights.astype(jnp.bfloat16)
            tops.append(top)
        top = jnp.concatenate(tops, 1)
        return top, (jnp.concatenate(factors, 1) if factors else None)

    def sum_up(c, top, factor):
        lanes = slice(c * wide, (c + 1) * wide)
        summed = dot(value_ext[c // per_group], p_buf[c % slots], ((1,), (0,)))[:TOP_ROW]
        if factor is not None:
            summed = summed + state_in[0:TOP_ROW, lanes] * factor
        if out_ref is None:
            state_out[0:TOP_ROW, lanes] = summed
            state_out[TOP_ROW : TOP_ROW + 1, lanes] = top
        else:
            finish(summed, top, c, heads, out_ref, log_ref)

    held = {}
    for t in range(chunks + 2):
        if t < chunks:
            score(t)
        if 0 <= t - 1 < chunks:
            held[t - 1] = weigh(t - 1)
        if 0 <= t - 2 < chunks:
            sum_up(t - 2, *held.pop(t - 2))


def finish(summed, top, c, heads, out_ref, log_ref):
    total = summed[HD : HD + 1]
    result = summed[:HD] * (1.0 / total)
    logs = top * SCALE + jnp.log(total)
    first = c * heads
    for h in range(heads):
        lanes = slice(h * HD, (h + 1) * HD)
        out_ref[:, (first + h) * HD : (first + h + 1) * HD] = result[:, lanes].T.astype(
            out_ref.dtype
        )
    log_ref[first : first + heads, :] = jnp.concatenate(
        [logs[:, h * HD : (h + 1) * HD] for h in range(heads)], 0
    )


def lane_row(rows):
    lane = lax.broadcasted_iota(jnp.int32, (rows, HD), 1)
    row = lax.broadcasted_iota(jnp.int32, (rows, HD), 0)
    return lane, row


def lowest_of(mark_ref):
    return jnp.max(mark_ref[...]).astype(jnp.int32)


def near_kernel(axis, mark_in, q_ref, own, other, state_out, mark, s_buf, p_buf):
    me = lax.axis_index(axis)
    rows = own.shape[0]
    lowest = lowest_of(mark_in)
    mark[...] = mark_in[...]
    lane, row = lane_row(rows)
    first_seen = jnp.where((me & 1) == 1, lowest - (me - 1) * rows, rows)
    other_flags = jnp.where((lane == 0) & (row < first_seen), 1.0, 0.0)
    own_flags = jnp.where((lane == row) & (row > 0), 1.0, 0.0)
    flags = jnp.concatenate([other_flags, own_flags], 0).astype(jnp.bfloat16)
    row_flags = jnp.where((lane == 0) | (lane > row), HIDDEN, 0.0).astype(jnp.bfloat16)
    run_chunks(
        q_ref, [other, own], flags, row_flags, None, state_out, s_buf, p_buf, None, None
    )


def far_kernel(axis, level, last, mark_in, q_ref, *refs):
    me = lax.axis_index(axis)
    count = 4
    blocks, state_in = refs[:count], refs[count]
    if last:
        state_out, (out_ref, log_ref, s_buf, p_buf) = None, refs[count + 1 :]
    else:
        (state_out, mark, s_buf, p_buf), out_ref, log_ref = refs[count + 1 :], None, None
        mark[...] = mark_in[...]
    rows = blocks[0].shape[0]
    lowest = lowest_of(mark_in)
    starts = [
        (who - level - first_reach(who & 1, turn)) * rows
        for turn in (0, 1)
        for who in (me, me ^ 1)
    ]
    needed = functools.reduce(jnp.logical_or, [s + rows > lowest for s in starts])

    @pl.when(needed)
    def _():
        lane, row = lane_row(rows)
        flags = jnp.concatenate(
            [jnp.where((lane == 0) & (row + s < lowest), 1.0, 0.0) for s in starts], 0
        ).astype(jnp.bfloat16)
        row_flags = jnp.where(lane == 0, HIDDEN, 0.0).astype(jnp.bfloat16)
        run_chunks(
            q_ref, blocks, flags, row_flags, state_in, state_out, s_buf, p_buf, out_ref, log_ref
        )

    @pl.when(jnp.logical_not(needed))
    def _():
        if last:
            wide = s_buf.shape[2]
            for c in range(q_ref.shape[1] // wide):
                lanes = slice(c * wide, (c + 1) * wide)
                top = state_in[TOP_ROW : TOP_ROW + 1, lanes]
                finish(state_in[0:TOP_ROW, lanes], top, c, wide // HD, out_ref, log_ref)
        else:
            state_out[...] = state_in[...]


def attend(kernel, mark, queries, blocks, state, last):
    rows, width = queries.shape
    heads = width // HD
    groups = blocks[0].shape[1] // (2 * HD)
    wide = HD * math.gcd(heads // groups, 4)
    keys = len(blocks) * rows
    operands = [mark, queries, *blocks]
    aliases = {}
    if state is not None:
        if not last:
            aliases = {len(operands): 0}
        operands.append(state)
    if last:
        out_shape = [
            jax.ShapeDtypeStruct((rows, width), jnp.bfloat16),
            jax.ShapeDtypeStruct((heads, rows), jnp.float32),
        ]
    else:
        out_shape = [
            jax.ShapeDtypeStruct((STATE_ROWS, width), jnp.float32),
            jax.ShapeDtypeStruct(MARK, jnp.float32),
        ]
    return pl.pallas_call(
        kernel,
        in_specs=[VMEM] * len(operands),
        out_specs=[VMEM] * len(out_shape),
        out_shape=out_shape,
        scratch_shapes=[
            pltpu.VMEM((2, keys, wide), jnp.float32),
            pltpu.VMEM((2, keys, wide), jnp.bfloat16),
        ],
        input_output_aliases=aliases,
        cost_estimate=pl.CostEstimate(
            flops=4 * keys * rows * width,
            bytes_accessed=rows * width * 2,
            transcendentals=keys * rows * heads,
        ),
        compiler_params=pltpu.CompilerParams(vmem_limit_bytes=12 << 20),
    )(*operands)


def fetch_kernel(axis, k_hbm, v_hbm, win_hbm, q_hbm, own_ref, mark_ref, q_ref, win_ref, sems):
    rows, width = k_hbm.shape
    copies = [
        pltpu.make_async_copy(k_hbm, own_ref.at[:, pl.ds(0, width)], sems.at[0]),
        pltpu.make_async_copy(v_hbm, own_ref.at[:, pl.ds(width, width)], sems.at[1]),
        pltpu.make_async_copy(win_hbm, win_ref, sems.at[2]),
        pltpu.make_async_copy(q_hbm, q_ref, sems.at[3]),
    ]
    for copy in copies:
        copy.start()
    for copy in copies:
        copy.wait()
    me = lax.axis_index(axis)
    lowest = jnp.maximum(me * rows - win_ref[me], 0)
    mark_ref[...] = jnp.full(mark_ref.shape, lowest.astype(jnp.float32))


def fetched(axis, queries, keys, values, windows):
    rows, width = keys.shape
    sources = [
        pltpu.with_memory_space_constraint(x, pltpu.HBM) for x in (keys, values, windows, queries)
    ]
    return pl.pallas_call(
        functools.partial(fetch_kernel, axis),
        in_specs=[HBM] * 4,
        out_specs=[VMEM] * 3,
        out_shape=[
            jax.ShapeDtypeStruct((rows, 2 * width), keys.dtype),
            jax.ShapeDtypeStruct(MARK, jnp.float32),
            jax.ShapeDtypeStruct(queries.shape, queries.dtype),
        ],
        scratch_shapes=[
            pltpu.SMEM(windows.shape, windows.dtype),
            pltpu.SemaphoreType.DMA((4,)),
        ],
        compiler_params=SMALL,
    )(*sources)


def tied(block, earlier):
    def kernel(block_ref, earlier_ref, out_ref):
        pass

    return pl.pallas_call(
        kernel,
        in_specs=[VMEM, VMEM],
        out_specs=VMEM,
        out_shape=jax.ShapeDtypeStruct(block.shape, block.dtype),
        input_output_aliases={0: 0},
        compiler_params=SMALL,
    )(block, earlier)


def on_device(queries, keys, values, windows):
    axis = "section"
    reach = lax.axis_size(axis) // 2
    own, mark, queries = fetched(axis, queries, keys, values, windows)
    other = swapped(own, axis)
    arrived = [shifted(own, axis, [first_reach(core, turn) for core in (0, 1)]) for turn in (0, 1)]
    state, mark = attend(
        functools.partial(near_kernel, axis), mark, queries, [own, other], None, False
    )
    for level in range(0, reach, 4):
        last = level + 4 >= reach
        blocks, later = [], []
        for block in arrived:
            block = tied(block, mark)
            if not last:
                later.append(shifted(block, axis, (4, 4)))
            blocks += [block, swapped(block, axis)]
        result = attend(
            functools.partial(far_kernel, axis, level, last),
            mark,
            queries,
            blocks,
            state,
            last,
        )
        arrived = later
        state, mark = result
    return result[0], result[1].T


def solution(mesh):
    placed = (
        P(("groups", "section"), None),
        P(("groups", "section"), None),
        P(("groups", "section"), None),
        P("groups"),
    )
    return jax.shard_map(
        on_device,
        mesh=mesh,
        in_specs=placed,
        out_specs=(P(("groups", "section"), None), P(("groups", "section"), None)),
        check_vma=False,
    )
```

```python
import functools
import math

import jax
import jax.numpy as jnp
from jax import lax
from jax.experimental import pallas as pl
from jax.experimental.pallas import tpu as pltpu
from jax.sharding import PartitionSpec as P

HD = 128
SCALE = HD ** (-0.5)
TO_EXP2 = SCALE * math.log2(math.e)
HIDDEN = -1e30
SUM_ROWS = 8
STATE_ROWS = HD + 2 * SUM_ROWS
TOP_ROW = HD + SUM_ROWS
TILE = 64
VMEM = pl.BlockSpec(memory_space=pltpu.VMEM)
SMALL = pltpu.CompilerParams(vmem_limit_bytes=1 << 20)
HBM = pl.BlockSpec(memory_space=pltpu.HBM)
MARK = (8, HD)
LAST = "last"


def shifted(block, axis, distance):
    size = lax.axis_size(axis)
    return lax.ppermute(block, axis, [(i, (i + distance) % size) for i in range(size)])


def swapped(block, axis):
    return lax.ppermute(block, axis, [(i ^ 1, i) for i in range(lax.axis_size(axis))])


def dot(left, right, dims):
    return lax.dot_general(left, right, (dims, ((), ())), preferred_element_type=jnp.float32)


def run_chunks(q_ref, blocks, flags, row_flags, state_in, state_out, s_buf, p_buf, outs):
    rows, width = q_ref.shape
    groups = blocks[0].shape[1] // (2 * HD)
    slots, keys, wide = s_buf.shape
    heads = wide // HD
    chunks = width // wide
    per_group = chunks // groups
    row_part = jnp.concatenate([row_flags] * heads, 0)
    ones = jnp.ones((2 * SUM_ROWS, keys), jnp.bfloat16)
    key_ext, value_ext = [], []
    for g in range(groups):
        key_rows = jnp.concatenate([b[:, g * HD : (g + 1) * HD] for b in blocks], 0)
        value_rows = jnp.concatenate(
            [b[:, (groups + g) * HD : (groups + g + 1) * HD] for b in blocks], 0
        )
        key_ext.append(jnp.concatenate([key_rows, flags], 1))
        value_ext.append(jnp.concatenate([value_rows.T, ones], 0))

    def score(c):
        parts = [q_ref[:, c * wide + h * HD : c * wide + (h + 1) * HD] for h in range(heads)]
        query_rows = jnp.concatenate([jnp.concatenate(parts, 0), row_part], 1)
        s_buf[c % slots] = dot(key_ext[c // per_group], query_rows, ((1,), (1,)))

    def weigh(c):
        slot, step = c % slots, wide
        tops, factors = [], []
        for j in range(0, wide, step):
            tiles = [
                (k, slice(j, j + step)) for k in range(0, keys, TILE)
            ]
            top = None
            for k, lanes in tiles:
                part = s_buf[slot, k : k + TILE, lanes].reshape(TILE // 8, 8, step)
                part = jnp.max(part, 0)
                top = part if top is None else jnp.maximum(top, part)
            top = jnp.max(top, 0, keepdims=True)
            if state_in is not None:
                old = state_in[TOP_ROW : TOP_ROW + 1, c * wide + j : c * wide + j + step]
                top = jnp.maximum(top, old)
                factors.append(jnp.exp2((old - top) * TO_EXP2))
            for k, lanes in tiles:
                weights = jnp.exp2((s_buf[slot, k : k + TILE, lanes] - top) * TO_EXP2)
                p_buf[slot, k : k + TILE, lanes] = weights.astype(jnp.bfloat16)
            tops.append(top)
        top = jnp.concatenate(tops, 1)
        return top, (jnp.concatenate(factors, 1) if factors else None)

    def sum_up(c, top, factor):
        lanes = slice(c * wide, (c + 1) * wide)
        summed = dot(value_ext[c // per_group], p_buf[c % slots], ((1,), (0,)))[:TOP_ROW]
        if factor is not None:
            summed = summed + state_in[0:TOP_ROW, lanes] * factor
        if outs is None:
            state_out[0:TOP_ROW, lanes] = summed
            state_out[TOP_ROW : TOP_ROW + 1, lanes] = top
        else:
            finish(summed, top, c, heads, *outs)

    held = {}
    for t in range(chunks + 2):
        if t < chunks:
            score(t)
        if 0 <= t - 1 < chunks:
            held[t - 1] = weigh(t - 1)
        if 0 <= t - 2 < chunks:
            sum_up(t - 2, *held.pop(t - 2))


def finish(summed, top, c, heads, out_ref, log_ref):
    total = summed[HD : HD + 1]
    result = summed[:HD] * (1.0 / total)
    logs = top * SCALE + jnp.log(total)
    first = c * heads
    for h in range(heads):
        lanes = slice(h * HD, (h + 1) * HD)
        out_ref[:, (first + h) * HD : (first + h + 1) * HD] = result[:, lanes].T.astype(
            out_ref.dtype
        )
    log_ref[first : first + heads, :] = jnp.concatenate(
        [logs[:, h * HD : (h + 1) * HD] for h in range(heads)], 0
    )


def lane_row(rows):
    lane = lax.broadcasted_iota(jnp.int32, (rows, HD), 1)
    row = lax.broadcasted_iota(jnp.int32, (rows, HD), 0)
    return lane, row


def lowest_of(mark_ref):
    return jnp.max(mark_ref[...]).astype(jnp.int32)


def near_kernel(axis, mark_in, q_ref, own, other, state_out, mark, s_buf, p_buf):
    me = lax.axis_index(axis)
    rows = own.shape[0]
    lowest = lowest_of(mark_in)
    mark[...] = mark_in[...]
    lane, row = lane_row(rows)
    first_seen = jnp.where((me & 1) == 1, lowest - (me - 1) * rows, rows)
    other_flags = jnp.where((lane == 0) & (row < first_seen), 1.0, 0.0)
    own_flags = jnp.where((lane == row) & (row > 0), 1.0, 0.0)
    flags = jnp.concatenate([other_flags, own_flags], 0).astype(jnp.bfloat16)
    row_flags = jnp.where((lane == 0) | (lane > row), HIDDEN, 0.0).astype(jnp.bfloat16)
    run_chunks(
        q_ref, [other, own], flags, row_flags, None, state_out, s_buf, p_buf, None
    )


def any_seen(distances, me, rows, lowest):
    starts = [(who - d) * rows for d in distances for who in (me, me ^ 1)]
    return functools.reduce(jnp.logical_or, [s + rows > lowest for s in starts]), starts


def finish_all(state, wide, out_ref, log_ref):
    for c in range(state.shape[1] // wide):
        lanes = slice(c * wide, (c + 1) * wide)
        top = state[TOP_ROW : TOP_ROW + 1, lanes]
        finish(state[0:TOP_ROW, lanes], top, c, wide // HD, out_ref, log_ref)


def write_out(out_buf, out_hbm, sem):
    copy = pltpu.make_async_copy(out_buf, out_hbm, sem)
    copy.start()
    copy.wait()


def far_kernel(axis, distances, later, mark_in, q_ref, *refs):
    me = lax.axis_index(axis)
    count = 2 * len(distances)
    blocks, state_in = refs[:count], refs[count]
    rows = blocks[0].shape[0]
    lowest = lowest_of(mark_in)
    needed, starts = any_seen(distances, me, rows, lowest)
    last = later == LAST
    refs = refs[count + 1 :]
    state_out, outs = None, None
    if last:
        log_in, out_hbm, log_ref, s_buf, p_buf, out_buf, sem = refs[1:]
        outs = (out_buf, log_ref)
    elif later:
        state_out, mark, out_hbm, log_ref, s_buf, p_buf, out_buf, sem = refs
    else:
        state_out, mark, s_buf, p_buf = refs
    if not last:
        mark[...] = mark_in[...]

    @pl.when(needed)
    def _():
        lane, row = lane_row(rows)
        flags = jnp.concatenate(
            [jnp.where((lane == 0) & (row + s < lowest), 1.0, 0.0) for s in starts], 0
        ).astype(jnp.bfloat16)
        row_flags = jnp.where(lane == 0, HIDDEN, 0.0).astype(jnp.bfloat16)
        run_chunks(q_ref, blocks, flags, row_flags, state_in, state_out, s_buf, p_buf, outs)
        if last:
            write_out(out_buf, out_hbm, sem)

    @pl.when(jnp.logical_not(needed))
    def _():
        if last:
            log_ref[...] = log_in[...]
        else:
            state_out[...] = state_in[...]

    if later and not last:
        more, _ = any_seen(later, me, rows, lowest)

        @pl.when(jnp.logical_not(more))
        def _():
            finish_all(state_out, s_buf.shape[2], out_buf, log_ref)
            write_out(out_buf, out_hbm, sem)


def attend(kernel, mark, queries, blocks, state, later):
    rows, width = queries.shape
    heads = width // HD
    groups = blocks[0].shape[1] // (2 * HD)
    wide = HD * math.gcd(heads // groups, 4)
    keys = len(blocks) * rows
    operands = [mark, queries, *blocks, *state]
    in_specs = [VMEM] * len(operands)
    results = [
        jax.ShapeDtypeStruct((rows, width), jnp.bfloat16),
        jax.ShapeDtypeStruct((heads, rows), jnp.float32),
    ]
    states = [
        jax.ShapeDtypeStruct((STATE_ROWS, width), jnp.float32),
        jax.ShapeDtypeStruct(MARK, jnp.float32),
    ]
    scratch = [
        pltpu.VMEM((2, keys, wide), jnp.float32),
        pltpu.VMEM((2, keys, wide), jnp.bfloat16),
    ]
    at = 2 + len(blocks)
    out_shape, out_specs, aliases = states, [VMEM] * 2, {at: 0} if state else {}
    if later:
        scratch += [pltpu.VMEM((rows, width), jnp.bfloat16), pltpu.SemaphoreType.DMA(())]
        if later == LAST:
            out_shape, out_specs, aliases = results, [HBM, VMEM], {at + 1: 0, at + 2: 1}
            in_specs[at + 1] = HBM
        else:
            out_shape, out_specs = states + results, [VMEM, VMEM, HBM, VMEM]
    return pl.pallas_call(
        kernel,
        in_specs=in_specs,
        out_specs=out_specs,
        out_shape=out_shape,
        scratch_shapes=scratch,
        input_output_aliases=aliases,
        cost_estimate=pl.CostEstimate(
            flops=4 * keys * rows * width,
            bytes_accessed=rows * width * 2,
            transcendentals=keys * rows * heads,
        ),
        compiler_params=pltpu.CompilerParams(vmem_limit_bytes=12 << 20),
    )(*operands)


def copy_all(copies):
    for copy in copies:
        copy.start()
    for copy in copies:
        copy.wait()


def own_kernel(k_hbm, v_hbm, own_ref, sems):
    width = k_hbm.shape[1]
    copy_all(
        [
            pltpu.make_async_copy(k_hbm, own_ref.at[:, pl.ds(0, width)], sems.at[0]),
            pltpu.make_async_copy(v_hbm, own_ref.at[:, pl.ds(width, width)], sems.at[1]),
        ]
    )


def query_kernel(axis, win_hbm, q_hbm, mark_ref, q_ref, win_ref, sems):
    copy_all(
        [
            pltpu.make_async_copy(win_hbm, win_ref, sems.at[0]),
            pltpu.make_async_copy(q_hbm, q_ref, sems.at[1]),
        ]
    )
    me = lax.axis_index(axis)
    lowest = jnp.maximum(me * q_ref.shape[0] - win_ref[me], 0)
    mark_ref[...] = jnp.full(mark_ref.shape, lowest.astype(jnp.float32))


def fetch(kernel, sources, out_shape, scratch):
    return pl.pallas_call(
        kernel,
        in_specs=[HBM] * len(sources),
        out_specs=[VMEM] * len(out_shape),
        out_shape=out_shape,
        scratch_shapes=scratch + [pltpu.SemaphoreType.DMA((2,))],
        compiler_params=SMALL,
    )(*[pltpu.with_memory_space_constraint(x, pltpu.HBM) for x in sources])


def fetched(axis, queries, keys, values, windows):
    rows, width = keys.shape
    (own,) = fetch(
        own_kernel, [keys, values], [jax.ShapeDtypeStruct((rows, 2 * width), keys.dtype)], []
    )
    mark, queries = fetch(
        functools.partial(query_kernel, axis),
        [windows, queries],
        [
            jax.ShapeDtypeStruct(MARK, jnp.float32),
            jax.ShapeDtypeStruct(queries.shape, queries.dtype),
        ],
        [pltpu.SMEM(windows.shape, windows.dtype)],
    )
    return own, mark, queries


def tied(block, earlier):
    def kernel(block_ref, earlier_ref, out_ref):
        pass

    return pl.pallas_call(
        kernel,
        in_specs=[VMEM, VMEM],
        out_specs=VMEM,
        out_shape=jax.ShapeDtypeStruct(block.shape, block.dtype),
        input_output_aliases={0: 0},
        compiler_params=SMALL,
    )(block, earlier)


def on_device(queries, keys, values, windows):
    axis = "section"
    reach = lax.axis_size(axis) // 2
    own, mark, queries = fetched(axis, queries, keys, values, windows)
    other = swapped(own, axis)
    held = {4: shifted(own, axis, 4), 2: shifted(own, axis, 2)}
    state, mark = attend(
        functools.partial(near_kernel, axis), mark, queries, [own, other], [], None
    )
    state = [state]
    rounds = [
        [d for d in (first + 2, first) if d <= reach] for first in range(2, reach + 1, 4)
    ]
    for index, distances in enumerate(rounds):
        blocks = []
        for d in distances:
            held[d] = tied(held[d], mark)
            if d + 4 <= reach:
                held[d + 4] = shifted(held[d], axis, 4)
            blocks += [held[d], swapped(held[d], axis)]
        later = LAST if index == len(rounds) - 1 else None
        if index == len(rounds) - 2:
            later = rounds[-1]
        result = attend(
            functools.partial(far_kernel, axis, distances, later),
            mark,
            queries,
            blocks,
            state,
            later,
        )
        if later != LAST:
            mark = result[1]
            state = [result[0], *result[2:]]
    return result[0], result[1].T


def solution(mesh):
    placed = (
        P(("groups", "section"), None),
        P(("groups", "section"), None),
        P(("groups", "section"), None),
        P("groups"),
    )
    return jax.shard_map(
        on_device,
        mesh=mesh,
        in_specs=placed,
        out_specs=(P(("groups", "section"), None), P(("groups", "section"), None)),
        check_vma=False,
    )
```

```python
import functools
import math

import jax
import jax.numpy as jnp
from jax import lax
from jax.experimental import pallas as pl
from jax.experimental.pallas import tpu as pltpu
from jax.sharding import PartitionSpec as P

HD = 128
SCALE = HD ** (-0.5)
TO_EXP2 = SCALE * math.log2(math.e)
HIDDEN = -1e30
SUM_ROWS = 8
STATE_ROWS = HD + 2 * SUM_ROWS
TOP_ROW = HD + SUM_ROWS
TILE = 64
VMEM = pl.BlockSpec(memory_space=pltpu.VMEM)
SMALL = pltpu.CompilerParams(vmem_limit_bytes=1 << 20)
HBM = pl.BlockSpec(memory_space=pltpu.HBM)
MARK = (8, HD)
LAST = "last"


def shifted(block, axis, distance):
    size = lax.axis_size(axis)
    return lax.ppermute(block, axis, [(i, (i + distance) % size) for i in range(size)])


def swapped(block, axis):
    return lax.ppermute(block, axis, [(i ^ 1, i) for i in range(lax.axis_size(axis))])


def dot(left, right, dims):
    return lax.dot_general(left, right, (dims, ((), ())), preferred_element_type=jnp.float32)


def run_chunks(q_ref, blocks, flags, row_flags, state_in, state_out, s_buf, p_buf, outs):
    rows, width = q_ref.shape
    groups = blocks[0].shape[1] // (2 * HD)
    slots, keys, wide = s_buf.shape
    heads = wide // HD
    chunks = width // wide
    per_group = chunks // groups
    row_part = jnp.concatenate([row_flags] * heads, 0)
    ones = jnp.ones((2 * SUM_ROWS, keys), jnp.bfloat16)
    key_ext, value_ext = [], []
    for g in range(groups):
        key_rows = jnp.concatenate([b[:, g * HD : (g + 1) * HD] for b in blocks], 0)
        value_rows = jnp.concatenate(
            [b[:, (groups + g) * HD : (groups + g + 1) * HD] for b in blocks], 0
        )
        key_ext.append(jnp.concatenate([key_rows, flags], 1))
        value_ext.append(jnp.concatenate([value_rows.T, ones], 0))

    def score(c):
        parts = [q_ref[:, c * wide + h * HD : c * wide + (h + 1) * HD] for h in range(heads)]
        query_rows = jnp.concatenate([jnp.concatenate(parts, 0), row_part], 1)
        s_buf[c % slots] = dot(key_ext[c // per_group], query_rows, ((1,), (1,)))

    def weigh(c):
        slot, step = c % slots, wide
        tops, factors = [], []
        for j in range(0, wide, step):
            tiles = [
                (k, slice(j, j + step)) for k in range(0, keys, TILE)
            ]
            top = None
            for k, lanes in tiles:
                part = s_buf[slot, k : k + TILE, lanes].reshape(TILE // 8, 8, step)
                part = jnp.max(part, 0)
                top = part if top is None else jnp.maximum(top, part)
            top = jnp.max(top, 0, keepdims=True)
            if state_in is not None:
                old = state_in[TOP_ROW : TOP_ROW + 1, c * wide + j : c * wide + j + step]
                top = jnp.maximum(top, old)
                factors.append(jnp.exp2((old - top) * TO_EXP2))
            for k, lanes in tiles:
                weights = jnp.exp2((s_buf[slot, k : k + TILE, lanes] - top) * TO_EXP2)
                p_buf[slot, k : k + TILE, lanes] = weights.astype(jnp.bfloat16)
            tops.append(top)
        top = jnp.concatenate(tops, 1)
        return top, (jnp.concatenate(factors, 1) if factors else None)

    def sum_up(c, top, factor):
        lanes = slice(c * wide, (c + 1) * wide)
        summed = dot(value_ext[c // per_group], p_buf[c % slots], ((1,), (0,)))[:TOP_ROW]
        if factor is not None:
            summed = summed + state_in[0:TOP_ROW, lanes] * factor
        if outs is None:
            state_out[0:TOP_ROW, lanes] = summed
            state_out[TOP_ROW : TOP_ROW + 1, lanes] = top
        else:
            finish(summed, top, c, heads, *outs)

    held = {}
    for t in range(chunks + 2):
        if t < chunks:
            score(t)
        if 0 <= t - 1 < chunks:
            held[t - 1] = weigh(t - 1)
        if 0 <= t - 2 < chunks:
            sum_up(t - 2, *held.pop(t - 2))


def finish(summed, top, c, heads, out_ref, log_ref):
    total = summed[HD : HD + 1]
    result = summed[:HD] * (1.0 / total)
    logs = top * SCALE + jnp.log(total)
    first = c * heads
    for h in range(heads):
        lanes = slice(h * HD, (h + 1) * HD)
        out_ref[:, (first + h) * HD : (first + h + 1) * HD] = result[:, lanes].T.astype(
            out_ref.dtype
        )
    log_ref[first : first + heads, :] = jnp.concatenate(
        [logs[:, h * HD : (h + 1) * HD] for h in range(heads)], 0
    )


def lane_row(rows):
    lane = lax.broadcasted_iota(jnp.int32, (rows, HD), 1)
    row = lax.broadcasted_iota(jnp.int32, (rows, HD), 0)
    return lane, row


def lowest_of(mark_ref):
    return jnp.max(mark_ref[...]).astype(jnp.int32)


def near_kernel(axis, mark_in, q_ref, own, other, state_out, mark, s_buf, p_buf):
    me = lax.axis_index(axis)
    rows = own.shape[0]
    lowest = lowest_of(mark_in)
    mark[...] = mark_in[...]
    lane, row = lane_row(rows)
    first_seen = jnp.where((me & 1) == 1, lowest - (me - 1) * rows, rows)
    other_flags = jnp.where((lane == 0) & (row < first_seen), 1.0, 0.0)
    own_flags = jnp.where((lane == row) & (row > 0), 1.0, 0.0)
    flags = jnp.concatenate([other_flags, own_flags], 0).astype(jnp.bfloat16)
    row_flags = jnp.where((lane == 0) | (lane > row), HIDDEN, 0.0).astype(jnp.bfloat16)
    run_chunks(
        q_ref, [other, own], flags, row_flags, None, state_out, s_buf, p_buf, None
    )


def any_seen(distances, me, rows, lowest):
    starts = [(who - d) * rows for d in distances for who in (me, me ^ 1)]
    return functools.reduce(jnp.logical_or, [s + rows > lowest for s in starts]), starts


def finish_all(state, wide, out_ref, log_ref):
    for c in range(state.shape[1] // wide):
        lanes = slice(c * wide, (c + 1) * wide)
        top = state[TOP_ROW : TOP_ROW + 1, lanes]
        finish(state[0:TOP_ROW, lanes], top, c, wide // HD, out_ref, log_ref)


def write_out(buffers, results, sems):
    copy_all(
        [pltpu.make_async_copy(x, y, sems.at[i]) for i, (x, y) in enumerate(zip(buffers, results))]
    )


def far_kernel(axis, distances, later, mark_in, q_ref, *refs):
    me = lax.axis_index(axis)
    count = 2 * len(distances)
    blocks, state_in = refs[:count], refs[count]
    rows = blocks[0].shape[0]
    lowest = lowest_of(mark_in)
    needed, starts = any_seen(distances, me, rows, lowest)
    last = later == LAST
    refs = refs[count + 1 :]
    state_out, outs = None, None
    if last:
        out_hbm, log_hbm, s_buf, p_buf, out_buf, log_buf, sems = refs[2:]
        outs = (out_buf, log_buf)
    elif later:
        state_out, mark, out_hbm, log_hbm, s_buf, p_buf, out_buf, log_buf, sems = refs
    else:
        state_out, mark, s_buf, p_buf = refs
    if not last:
        mark[...] = mark_in[...]

    @pl.when(needed)
    def _():
        lane, row = lane_row(rows)
        flags = jnp.concatenate(
            [jnp.where((lane == 0) & (row + s < lowest), 1.0, 0.0) for s in starts], 0
        ).astype(jnp.bfloat16)
        row_flags = jnp.where(lane == 0, HIDDEN, 0.0).astype(jnp.bfloat16)
        run_chunks(q_ref, blocks, flags, row_flags, state_in, state_out, s_buf, p_buf, outs)
        if last:
            write_out((out_buf, log_buf), (out_hbm, log_hbm), sems)

    if not last:

        @pl.when(jnp.logical_not(needed))
        def _():
            state_out[...] = state_in[...]

    if later and not last:
        more, _ = any_seen(later, me, rows, lowest)

        @pl.when(jnp.logical_not(more))
        def _():
            finish_all(state_out, s_buf.shape[2], out_buf, log_buf)
            write_out((out_buf, log_buf), (out_hbm, log_hbm), sems)


def attend(kernel, mark, queries, blocks, state, later):
    rows, width = queries.shape
    heads = width // HD
    groups = blocks[0].shape[1] // (2 * HD)
    wide = HD * math.gcd(heads // groups, 4)
    keys = len(blocks) * rows
    operands = [mark, queries, *blocks, *state]
    in_specs = [VMEM] * len(operands)
    results = [
        jax.ShapeDtypeStruct((rows, width), jnp.bfloat16),
        jax.ShapeDtypeStruct((heads, rows), jnp.float32),
    ]
    states = [
        jax.ShapeDtypeStruct((STATE_ROWS, width), jnp.float32),
        jax.ShapeDtypeStruct(MARK, jnp.float32),
    ]
    scratch = [
        pltpu.VMEM((2, keys, wide), jnp.float32),
        pltpu.VMEM((2, keys, wide), jnp.bfloat16),
    ]
    at = 2 + len(blocks)
    out_shape, out_specs, aliases = states, [VMEM] * 2, {at: 0} if state else {}
    if later:
        scratch += [
            pltpu.VMEM((rows, width), jnp.bfloat16),
            pltpu.VMEM((heads, rows), jnp.float32),
            pltpu.SemaphoreType.DMA((2,)),
        ]
        if later == LAST:
            out_shape, out_specs, aliases = results, [HBM] * 2, {at + 1: 0, at + 2: 1}
            in_specs[at + 1 :] = [HBM] * 2
        else:
            out_shape, out_specs = states + results, [VMEM, VMEM, HBM, HBM]
    return pl.pallas_call(
        kernel,
        in_specs=in_specs,
        out_specs=out_specs,
        out_shape=out_shape,
        scratch_shapes=scratch,
        input_output_aliases=aliases,
        cost_estimate=pl.CostEstimate(
            flops=4 * keys * rows * width,
            bytes_accessed=rows * width * 2,
            transcendentals=keys * rows * heads,
        ),
        compiler_params=pltpu.CompilerParams(vmem_limit_bytes=12 << 20),
    )(*operands)


def copy_all(copies):
    for copy in copies:
        copy.start()
    for copy in copies:
        copy.wait()


def own_kernel(k_hbm, v_hbm, own_ref, sems):
    width = k_hbm.shape[1]
    copy_all(
        [
            pltpu.make_async_copy(k_hbm, own_ref.at[:, pl.ds(0, width)], sems.at[0]),
            pltpu.make_async_copy(v_hbm, own_ref.at[:, pl.ds(width, width)], sems.at[1]),
        ]
    )


def query_kernel(axis, win_hbm, q_hbm, mark_ref, q_ref, win_ref, sems):
    copy_all(
        [
            pltpu.make_async_copy(win_hbm, win_ref, sems.at[0]),
            pltpu.make_async_copy(q_hbm, q_ref, sems.at[1]),
        ]
    )
    me = lax.axis_index(axis)
    lowest = jnp.maximum(me * q_ref.shape[0] - win_ref[me], 0)
    mark_ref[...] = jnp.full(mark_ref.shape, lowest.astype(jnp.float32))


def fetch(kernel, sources, out_shape, scratch):
    return pl.pallas_call(
        kernel,
        in_specs=[HBM] * len(sources),
        out_specs=[VMEM] * len(out_shape),
        out_shape=out_shape,
        scratch_shapes=scratch + [pltpu.SemaphoreType.DMA((2,))],
        compiler_params=SMALL,
    )(*[pltpu.with_memory_space_constraint(x, pltpu.HBM) for x in sources])


def fetched(axis, queries, keys, values, windows):
    rows, width = keys.shape
    (own,) = fetch(
        own_kernel, [keys, values], [jax.ShapeDtypeStruct((rows, 2 * width), keys.dtype)], []
    )
    mark, queries = fetch(
        functools.partial(query_kernel, axis),
        [windows, queries],
        [
            jax.ShapeDtypeStruct(MARK, jnp.float32),
            jax.ShapeDtypeStruct(queries.shape, queries.dtype),
        ],
        [pltpu.SMEM(windows.shape, windows.dtype)],
    )
    return own, mark, queries


def tied(block, earlier):
    def kernel(block_ref, earlier_ref, out_ref):
        pass

    return pl.pallas_call(
        kernel,
        in_specs=[VMEM, VMEM],
        out_specs=VMEM,
        out_shape=jax.ShapeDtypeStruct(block.shape, block.dtype),
        input_output_aliases={0: 0},
        compiler_params=SMALL,
    )(block, earlier)


def on_device(queries, keys, values, windows):
    axis = "section"
    reach = lax.axis_size(axis) // 2
    own, mark, queries = fetched(axis, queries, keys, values, windows)
    other = swapped(own, axis)
    held = {4: shifted(own, axis, 4), 2: shifted(own, axis, 2)}
    state, mark = attend(
        functools.partial(near_kernel, axis), mark, queries, [own, other], [], None
    )
    state = [state]
    rounds = [
        [d for d in (first + 2, first) if d <= reach] for first in range(2, reach + 1, 4)
    ]
    for index, distances in enumerate(rounds):
        blocks = []
        for d in distances:
            held[d] = tied(held[d], mark)
            if d + 4 <= reach:
                held[d + 4] = shifted(held[d], axis, 4)
            blocks += [held[d], swapped(held[d], axis)]
        later = LAST if index == len(rounds) - 1 else None
        if index == len(rounds) - 2:
            later = rounds[-1]
        result = attend(
            functools.partial(far_kernel, axis, distances, later),
            mark,
            queries,
            blocks,
            state,
            later,
        )
        if later != LAST:
            mark = result[1]
            state = [result[0], *result[2:]]
    return result[0], result[1].T


def solution(mesh):
    placed = (
        P(("groups", "section"), None),
        P(("groups", "section"), None),
        P(("groups", "section"), None),
        P("groups"),
    )
    return jax.shard_map(
        on_device,
        mesh=mesh,
        in_specs=placed,
        out_specs=(P(("groups", "section"), None), P(("groups", "section"), None)),
        check_vma=False,
    )
```

```python
import functools
import math

import jax
import jax.numpy as jnp
from jax import lax
from jax.experimental import pallas as pl
from jax.experimental.pallas import tpu as pltpu
from jax.sharding import PartitionSpec as P

HD = 128
SCALE = HD ** (-0.5)
TO_EXP2 = SCALE * math.log2(math.e)
HIDDEN = -1e30
SUM_ROWS = 8
STATE_ROWS = HD + 2 * SUM_ROWS
TOP_ROW = HD + SUM_ROWS
TILE = 64
VMEM = pl.BlockSpec(memory_space=pltpu.VMEM)
SMALL = pltpu.CompilerParams(vmem_limit_bytes=1 << 20)
HBM = pl.BlockSpec(memory_space=pltpu.HBM)
MARK = (8, HD)
LAST = "last"


def shifted(block, axis, distance):
    size = lax.axis_size(axis)
    return lax.ppermute(block, axis, [(i, (i + distance) % size) for i in range(size)])


def swapped(block, axis):
    return lax.ppermute(block, axis, [(i ^ 1, i) for i in range(lax.axis_size(axis))])


def dot(left, right, dims):
    return lax.dot_general(left, right, (dims, ((), ())), preferred_element_type=jnp.float32)


def run_chunks(q_ref, blocks, flags, row_flags, state_in, state_out, s_buf, p_buf, outs):
    rows, width = q_ref.shape
    groups = blocks[0].shape[1] // (2 * HD)
    slots, keys, wide = s_buf.shape
    heads = wide // HD
    chunks = width // wide
    per_group = chunks // groups
    row_part = jnp.concatenate([row_flags] * heads, 0)
    ones = jnp.ones((2 * SUM_ROWS, keys), jnp.bfloat16)
    key_ext, value_ext = [], []
    for g in range(groups):
        key_rows = jnp.concatenate([b[:, g * HD : (g + 1) * HD] for b in blocks], 0)
        value_rows = jnp.concatenate(
            [b[:, (groups + g) * HD : (groups + g + 1) * HD] for b in blocks], 0
        )
        key_ext.append(jnp.concatenate([key_rows, flags], 1))
        value_ext.append(jnp.concatenate([value_rows.T, ones], 0))

    def score(c):
        parts = [q_ref[:, c * wide + h * HD : c * wide + (h + 1) * HD] for h in range(heads)]
        query_rows = jnp.concatenate([jnp.concatenate(parts, 0), row_part], 1)
        s_buf[c % slots] = dot(key_ext[c // per_group], query_rows, ((1,), (1,)))

    def weigh(c):
        slot, step = c % slots, wide
        tops, factors = [], []
        for j in range(0, wide, step):
            tiles = [
                (k, slice(j, j + step)) for k in range(0, keys, TILE)
            ]
            top = None
            for k, lanes in tiles:
                part = s_buf[slot, k : k + TILE, lanes].reshape(TILE // 8, 8, step)
                part = jnp.max(part, 0)
                top = part if top is None else jnp.maximum(top, part)
            top = jnp.max(top, 0, keepdims=True)
            if state_in is not None:
                old = state_in[TOP_ROW : TOP_ROW + 1, c * wide + j : c * wide + j + step]
                top = jnp.maximum(top, old)
                factors.append(jnp.exp2((old - top) * TO_EXP2))
            for k, lanes in tiles:
                weights = jnp.exp2((s_buf[slot, k : k + TILE, lanes] - top) * TO_EXP2)
                p_buf[slot, k : k + TILE, lanes] = weights.astype(jnp.bfloat16)
            tops.append(top)
        top = jnp.concatenate(tops, 1)
        return top, (jnp.concatenate(factors, 1) if factors else None)

    def sum_up(c, top, factor):
        lanes = slice(c * wide, (c + 1) * wide)
        summed = dot(value_ext[c // per_group], p_buf[c % slots], ((1,), (0,)))[:TOP_ROW]
        if factor is not None:
            summed = summed + state_in[0:TOP_ROW, lanes] * factor
        if outs is None:
            state_out[0:TOP_ROW, lanes] = summed
            state_out[TOP_ROW : TOP_ROW + 1, lanes] = top
        else:
            finish(summed, top, c, heads, *outs)

    held = {}
    for t in range(chunks + 2):
        if t < chunks:
            score(t)
        if 0 <= t - 1 < chunks:
            held[t - 1] = weigh(t - 1)
        if 0 <= t - 2 < chunks:
            sum_up(t - 2, *held.pop(t - 2))


def finish(summed, top, c, heads, out_ref, log_ref):
    total = summed[HD : HD + 1]
    result = summed[:HD] * (1.0 / total)
    logs = top * SCALE + jnp.log(total)
    first = c * heads
    for h in range(heads):
        lanes = slice(h * HD, (h + 1) * HD)
        out_ref[:, (first + h) * HD : (first + h + 1) * HD] = result[:, lanes].T.astype(
            out_ref.dtype
        )
    log_ref[first : first + heads, :] = jnp.concatenate(
        [logs[:, h * HD : (h + 1) * HD] for h in range(heads)], 0
    )


def lane_row(rows):
    lane = lax.broadcasted_iota(jnp.int32, (rows, HD), 1)
    row = lax.broadcasted_iota(jnp.int32, (rows, HD), 0)
    return lane, row


def lowest_of(mark_ref):
    return jnp.max(mark_ref[...]).astype(jnp.int32)


def near_kernel(axis, mark_in, q_ref, own, other, state_out, mark, s_buf, p_buf):
    me = lax.axis_index(axis)
    rows = own.shape[0]
    lowest = lowest_of(mark_in)
    mark[...] = mark_in[...]
    lane, row = lane_row(rows)
    first_seen = jnp.where((me & 1) == 1, lowest - (me - 1) * rows, rows)
    other_flags = jnp.where((lane == 0) & (row < first_seen), 1.0, 0.0)
    own_flags = jnp.where((lane == row) & (row > 0), 1.0, 0.0)
    flags = jnp.concatenate([other_flags, own_flags], 0).astype(jnp.bfloat16)
    row_flags = jnp.where((lane == 0) | (lane > row), HIDDEN, 0.0).astype(jnp.bfloat16)
    run_chunks(
        q_ref, [other, own], flags, row_flags, None, state_out, s_buf, p_buf, None
    )


def any_seen(distances, me, rows, lowest):
    starts = [(who - d) * rows for d in distances for who in (me, me ^ 1)]
    return functools.reduce(jnp.logical_or, [s + rows > lowest for s in starts]), starts


def finish_all(state, wide, out_ref, log_ref):
    for c in range(state.shape[1] // wide):
        lanes = slice(c * wide, (c + 1) * wide)
        top = state[TOP_ROW : TOP_ROW + 1, lanes]
        finish(state[0:TOP_ROW, lanes], top, c, wide // HD, out_ref, log_ref)


def write_out(buffers, results, sems):
    copy_all(
        [pltpu.make_async_copy(x, y, sems.at[i]) for i, (x, y) in enumerate(zip(buffers, results))]
    )


def far_kernel(axis, distances, later, mark_in, q_ref, *refs):
    me = lax.axis_index(axis)
    count = 2 * len(distances)
    blocks, state_in = refs[:count], refs[count]
    rows = blocks[0].shape[0]
    lowest = lowest_of(mark_in)
    needed, starts = any_seen(distances, me, rows, lowest)
    last = later == LAST
    refs = refs[count + 1 :]
    state_out, outs = None, None
    if last:
        out_hbm, log_hbm, s_buf, p_buf, out_buf, log_buf, sems = refs[2:]
        outs = (out_buf, log_buf)
    elif later:
        state_out, mark, out_hbm, log_hbm, s_buf, p_buf, out_buf, log_buf, sems = refs
    else:
        state_out, mark, s_buf, p_buf = refs
    if not last:
        mark[...] = mark_in[...]

    @pl.when(needed)
    def _():
        lane, row = lane_row(rows)
        flags = jnp.concatenate(
            [jnp.where((lane == 0) & (row + s < lowest), 1.0, 0.0) for s in starts], 0
        ).astype(jnp.bfloat16)
        row_flags = jnp.where(lane == 0, HIDDEN, 0.0).astype(jnp.bfloat16)
        run_chunks(q_ref, blocks, flags, row_flags, state_in, state_out, s_buf, p_buf, outs)
        if last:
            write_out((out_buf, log_buf), (out_hbm, log_hbm), sems)

    if not last:

        @pl.when(jnp.logical_not(needed))
        def _():
            state_out[...] = state_in[...]

    if later and not last:
        more, _ = any_seen(later, me, rows, lowest)

        @pl.when(jnp.logical_not(more))
        def _():
            finish_all(state_out, s_buf.shape[2], out_buf, log_buf)
            write_out((out_buf, log_buf), (out_hbm, log_hbm), sems)


def attend(kernel, mark, queries, blocks, state, later):
    rows, width = queries.shape
    heads = width // HD
    groups = blocks[0].shape[1] // (2 * HD)
    wide = HD * math.gcd(heads // groups, 8 if later == LAST else 4)
    keys = len(blocks) * rows
    operands = [mark, queries, *blocks, *state]
    in_specs = [VMEM] * len(operands)
    results = [
        jax.ShapeDtypeStruct((rows, width), jnp.bfloat16),
        jax.ShapeDtypeStruct((heads, rows), jnp.float32),
    ]
    states = [
        jax.ShapeDtypeStruct((STATE_ROWS, width), jnp.float32),
        jax.ShapeDtypeStruct(MARK, jnp.float32),
    ]
    scratch = [
        pltpu.VMEM((2, keys, wide), jnp.float32),
        pltpu.VMEM((2, keys, wide), jnp.bfloat16),
    ]
    at = 2 + len(blocks)
    out_shape, out_specs, aliases = states, [VMEM] * 2, {at: 0} if state else {}
    if later:
        scratch += [
            pltpu.VMEM((rows, width), jnp.bfloat16),
            pltpu.VMEM((heads, rows), jnp.float32),
            pltpu.SemaphoreType.DMA((2,)),
        ]
        if later == LAST:
            out_shape, out_specs, aliases = results, [HBM] * 2, {at + 1: 0, at + 2: 1}
            in_specs[at + 1 :] = [HBM] * 2
        else:
            out_shape, out_specs = states + results, [VMEM, VMEM, HBM, HBM]
    return pl.pallas_call(
        kernel,
        in_specs=in_specs,
        out_specs=out_specs,
        out_shape=out_shape,
        scratch_shapes=scratch,
        input_output_aliases=aliases,
        cost_estimate=pl.CostEstimate(
            flops=4 * keys * rows * width,
            bytes_accessed=rows * width * 2,
            transcendentals=keys * rows * heads,
        ),
        compiler_params=pltpu.CompilerParams(vmem_limit_bytes=12 << 20),
    )(*operands)


def copy_all(copies):
    for copy in copies:
        copy.start()
    for copy in copies:
        copy.wait()


def own_kernel(k_hbm, v_hbm, own_ref, sems):
    width = k_hbm.shape[1]
    copy_all(
        [
            pltpu.make_async_copy(k_hbm, own_ref.at[:, pl.ds(0, width)], sems.at[0]),
            pltpu.make_async_copy(v_hbm, own_ref.at[:, pl.ds(width, width)], sems.at[1]),
        ]
    )


def query_kernel(axis, win_hbm, q_hbm, mark_ref, q_ref, win_ref, sems):
    copy_all(
        [
            pltpu.make_async_copy(win_hbm, win_ref, sems.at[0]),
            pltpu.make_async_copy(q_hbm, q_ref, sems.at[1]),
        ]
    )
    me = lax.axis_index(axis)
    lowest = jnp.maximum(me * q_ref.shape[0] - win_ref[me], 0)
    mark_ref[...] = jnp.full(mark_ref.shape, lowest.astype(jnp.float32))


def fetch(kernel, sources, out_shape, scratch):
    return pl.pallas_call(
        kernel,
        in_specs=[HBM] * len(sources),
        out_specs=[VMEM] * len(out_shape),
        out_shape=out_shape,
        scratch_shapes=scratch + [pltpu.SemaphoreType.DMA((2,))],
        compiler_params=SMALL,
    )(*[pltpu.with_memory_space_constraint(x, pltpu.HBM) for x in sources])


def fetched(axis, queries, keys, values, windows):
    rows, width = keys.shape
    (own,) = fetch(
        own_kernel, [keys, values], [jax.ShapeDtypeStruct((rows, 2 * width), keys.dtype)], []
    )
    mark, queries = fetch(
        functools.partial(query_kernel, axis),
        [windows, queries],
        [
            jax.ShapeDtypeStruct(MARK, jnp.float32),
            jax.ShapeDtypeStruct(queries.shape, queries.dtype),
        ],
        [pltpu.SMEM(windows.shape, windows.dtype)],
    )
    return own, mark, queries


def tied(block, earlier):
    def kernel(block_ref, earlier_ref, out_ref):
        pass

    return pl.pallas_call(
        kernel,
        in_specs=[VMEM, VMEM],
        out_specs=VMEM,
        out_shape=jax.ShapeDtypeStruct(block.shape, block.dtype),
        input_output_aliases={0: 0},
        compiler_params=SMALL,
    )(block, earlier)


def on_device(queries, keys, values, windows):
    axis = "section"
    reach = lax.axis_size(axis) // 2
    own, mark, queries = fetched(axis, queries, keys, values, windows)
    other = swapped(own, axis)
    held = {4: shifted(own, axis, 4), 2: shifted(own, axis, 2)}
    state, mark = attend(
        functools.partial(near_kernel, axis), mark, queries, [own, other], [], None
    )
    state = [state]
    rounds = [
        [d for d in (first + 2, first) if d <= reach] for first in range(2, reach + 1, 4)
    ]
    for index, distances in enumerate(rounds):
        blocks = []
        for d in distances:
            held[d] = tied(held[d], mark)
            if d + 4 <= reach:
                held[d + 4] = shifted(held[d], axis, 4)
            blocks += [held[d], swapped(held[d], axis)]
        later = LAST if index == len(rounds) - 1 else None
        if index == len(rounds) - 2:
            later = rounds[-1]
        result = attend(
            functools.partial(far_kernel, axis, distances, later),
            mark,
            queries,
            blocks,
            state,
            later,
        )
        if later != LAST:
            mark = result[1]
            state = [result[0], *result[2:]]
    return result[0], result[1].T


def solution(mesh):
    placed = (
        P(("groups", "section"), None),
        P(("groups", "section"), None),
        P(("groups", "section"), None),
        P("groups"),
    )
    return jax.shard_map(
        on_device,
        mesh=mesh,
        in_specs=placed,
        out_specs=(P(("groups", "section"), None), P(("groups", "section"), None)),
        check_vma=False,
    )
```
